32 devices in a mesh: dp: 8 (over z, core), pos: 4 (over y, x).
Axes of the slice: x: 2, y: 2, z: 4, core: 2. Of those that a mesh axis runs over, the one named last changes fastest.
Arguments:
- tokens_in: bfloat16 [32, 256, 768], P(('dp', 'pos')), may hold values from -6 to 6
- doc_lengths: int32 [32, 3], P(('dp', 'pos')), may hold values from 1 to 240, 256 in all within a row
- norm_gains: float32 [2, 2, 768], replicated, may hold values from 0.25 to 1.75
- in_proj: bfloat16 [2, 768, 2304], P(None, ('dp', 'pos')), may hold values from -0.21875 to 0.21875
- short_filter: float32 [2, 3, 2304], replicated, may hold values from -3 to 3
- filter_in: float32 [2, 33, 64], replicated, may hold values from -1 to 1
- filter_biases: float32 [2, 2, 64], replicated, may hold values from -4 to 4
- sine_freq: float32 [2, 2, 64], replicated, may hold values from 2 to 12
- filter_mid: float32 [2, 64, 64], replicated, may hold values from -0.75 to 0.75
- filter_out: float32 [2, 64, 768], replicated, may hold values from -0.09375 to 0.09375
- decay_rates: float32 [2, 768], replicated, may hold values from 1 to 30
- skip_bias: float32 [2, 768], replicated, may hold values from -4 to 4
- out_proj: bfloat16 [2, 768, 768], P(None, ('dp', 'pos')), may hold values from -0.21875 to 0.21875
- mlp_up: bfloat16 [2, 768, 3072], P(None, ('dp', 'pos')), may hold values from -0.21875 to 0.21875
- mlp_down: bfloat16 [2, 3072, 768], P(None, ('dp', 'pos')), may hold values from -0.109375 to 0.109375
- out_grad: bfloat16 [32, 256, 768], P(('dp', 'pos')), may hold values from -6 to 6
Outputs:
- tokens_out: bfloat16 [32, 256, 768], P(('dp', 'pos'))
- tokens_grad: float32 [32, 256, 768], P(('dp', 'pos'))
- grad_norm_gains: float32 [2, 2, 768], P(None, None, ('dp', 'pos'))
- grad_in_proj: float32 [2, 768, 2304], P(None, ('dp', 'pos'))
- grad_short_filter: float32 [2, 3, 2304], P(None, None, ('dp', 'pos'))
- grad_filter_in: float32 [2, 33, 64], replicated
- grad_filter_biases: float32 [2, 2, 64], replicated
- grad_sine_freq: float32 [2, 2, 64], replicated
- grad_filter_mid: float32 [2, 64, 64], replicated
- grad_filter_out: float32 [2, 64, 768], replicated
- grad_decay_rates: float32 [2, 768], replicated
- grad_skip_bias: float32 [2, 768], P(None, ('dp', 'pos'))
- grad_out_proj: float32 [2, 768, 768], P(None, ('dp', 'pos'))
- grad_mlp_up: float32 [2, 768, 3072], P(None, ('dp', 'pos'))
- grad_mlp_down: float32 [2, 3072, 768], P(None, ('dp', 'pos'))
The draws below stay inside these ranges and needn't reach their ends.
Inputs may be any that keep to these rules, and one draw needn't show every extreme that they name: `doc_lengths`: the 3 lengths of a row sum to 256; one of them is 240 in every row.
All inputs are finite; a program needn't handle non-finite values.
Results may differ from the reference program's by a relative error of at most 0.033.
Values may be sent and summed in bfloat16 or wider, within the bound.
No kernel may reach another device: no remote copies, remote signals or barrier semaphores. Data moves between devices by JAX's collectives and lax.ppermute only.
A program may use at most 256 MiB of HBM per device.

```python
import math
import jax
import jax.numpy as jnp
import numpy as np
from jax import lax

D = 768
FF = 3072
FH = 64
EMB = 33
ROW_LEN = 256
LAYERS = 2
DOCS = 3
ROWS = 32


def steps_of(stream_key, extent, cuts, least, high):
    gain, own = 1.0, jax.random.fold_in(stream_key, 6)
    for position, blocks in cuts:
        draws = jnp.exp(jax.random.uniform(jax.random.fold_in(own, position), (blocks,), jnp.float32, least / len(cuts), high / len(cuts)))
        gain = gain * jnp.repeat(draws, extent[position] // blocks).reshape([-1 if axis == position else 1 for axis in range(len(extent))])
    return gain


def profile(number_of, total, bound, lean):
    loads = [(1 << 20) // math.isqrt(grade ** lean) + 1 for grade in range(2, number_of + 1)]
    surplus, holding = total - bound - (number_of - 1), [1] * (number_of - 1)
    while surplus > 0:
        free = [i for i in range(number_of - 1) if holding[i] < bound]
        mass, left = sum([loads[i] for i in free]), surplus
        for i in free:
            more = min(bound - holding[i], max(1, left * loads[i] // mass), surplus)
            holding[i] = holding[i] + more
            surplus = surplus - more
    return np.array([bound] + holding)


def ragged_sizes(stream_key, count, total, bound, slope):
    if count == 2:
        one = jax.random.randint(stream_key, (), max(1, total - bound), min(bound, total - 1) + 1)
        return jnp.stack([one, total - one])
    tallies = jnp.asarray(profile(count, total, bound, slope), jnp.int32)
    twos = (count - 1) // 2
    giver, receiver = tallies[1:1 + 2 * twos:2], tallies[2:2 + 2 * twos:2]
    room = jnp.minimum(giver - 1, bound - receiver)
    moved = jax.random.randint(jax.random.fold_in(stream_key, 1), (twos,), 0, 1 << 20) % (room + 1)
    tallies = tallies.at[1:1 + 2 * twos:2].set(giver - moved).at[2:2 + 2 * twos:2].set(receiver + moved)
    return tallies[jax.random.permutation(jax.random.fold_in(stream_key, 2), count)]


def scatter_about(key, shape, scale, reach, split=(), held_as=jnp.bfloat16):
    factor_of = steps_of(key, shape, split, -0.22, 0.18) if split else 1.0
    values = jax.random.normal(key, shape, jnp.float32) * scale * factor_of
    return jnp.minimum(jnp.maximum(values, -reach), reach).astype(held_as)


def setup_inputs(seed: int = 0) -> dict:
    key_of = jax.random.split(jax.random.key(seed), 17)
    return {
        "tokens_in": scatter_about(key_of[0], (ROWS, ROW_LEN, D), 1.0, 6.0, ((0, 32),)),
        "doc_lengths": jax.vmap(lambda own: ragged_sizes(own, DOCS, ROW_LEN, ROW_LEN - ROW_LEN // 16, 1))(jax.random.split(key_of[1], ROWS)).reshape((ROWS, DOCS)).astype(jnp.int32),
        "norm_gains": jnp.clip(1.0 + 0.15 * jax.random.normal(key_of[2], (LAYERS, 2, D), jnp.float32), 0.25, 1.75),
        "in_proj": scatter_about(key_of[3], (LAYERS, D, 3 * D), D ** -0.5, 0.21875, ((1, 32),)),
        "short_filter": scatter_about(key_of[4], (LAYERS, 3, 3 * D), 0.6, 3.0, (), jnp.float32),
        "filter_in": scatter_about(key_of[5], (LAYERS, EMB, FH), EMB ** -0.5, 1.0, (), jnp.float32),
        "filter_biases": scatter_about(key_of[6], (LAYERS, 2, FH), 1.0, 4.0, (), jnp.float32),
        "sine_freq": jnp.clip(jnp.exp(jax.random.uniform(key_of[7], (LAYERS, 2, FH), jnp.float32, math.log(2.0), math.log(12.0))), 2.0, 12.0),
        "filter_mid": scatter_about(key_of[8], (LAYERS, FH, FH), FH ** -0.5, 0.75, (), jnp.float32),
        "filter_out": scatter_about(key_of[9], (LAYERS, FH, D), (FH * FH) ** -0.5, 0.09375, (), jnp.float32),
        "decay_rates": jnp.clip(jnp.exp(jax.random.uniform(key_of[10], (LAYERS, D), jnp.float32, math.log(1.0), math.log(30.0))), 1.0, 30.0),
        "skip_bias": scatter_about(key_of[11], (LAYERS, D), 1.0, 4.0, (), jnp.float32),
        "out_proj": scatter_about(key_of[12], (LAYERS, D, D), D ** -0.5, 0.21875, ((1, 32),)),
        "mlp_up": scatter_about(key_of[13], (LAYERS, D, FF), D ** -0.5, 0.21875, ((1, 32),)),
        "mlp_down": scatter_about(key_of[14], (LAYERS, FF, D), FF ** -0.5, 0.109375, ((1, 32),)),
        "out_grad": scatter_about(key_of[15], (ROWS, ROW_LEN, D), 1.0, 6.0, ((0, 32),)),
    }


highest = lax.Precision.HIGHEST
norm_epsilon = 1e-05

@jax.custom_vjp
def low(v):
    return lax.optimization_barrier(v.astype(jnp.bfloat16)).astype(jnp.float32)

@jax.custom_vjp
def low_back(v):
    return v

def low_keep(v):
    return (low(v), None)

def low_pass(kept, grad):
    return (grad,)

def back_keep(v):
    return (v, None)

def back_low(kept, grad):
    return (low(grad),)
low.defvjp(low_keep, low_pass)
low_back.defvjp(back_keep, back_low)

def layer_norm(values, gain_vec):
    centered = values - lax.optimization_barrier(jnp.mean(values, axis=-1, keepdims=True))
    inv_scale = lax.rsqrt(lax.optimization_barrier(jnp.mean(centered * centered, axis=-1, keepdims=True)) + norm_epsilon)
    return centered * inv_scale * gain_vec

def segments(doc_lengths, length):
    doc_ends = jnp.cumsum(doc_lengths, axis=-1)
    doc_starts = doc_ends - doc_lengths
    places = jnp.arange(length, dtype=jnp.int32)
    return lax.optimization_barrier(jnp.sum((places[None, :, None] >= doc_starts[:, None, :]).astype(jnp.int32), axis=-1)) - 1

def short_mix(projected, short_taps, segment):
    mixed_sum = short_taps[0] * projected
    for offset in (1, 2):
        shifted = jnp.pad(projected[:, :-offset], ((0, 0), (offset, 0), (0, 0)))
        joined = jnp.pad(segment[:, offset:] == segment[:, :-offset], ((0, 0), (offset, 0)))
        mixed_sum = mixed_sum + short_taps[offset] * shifted * joined[..., None].astype(projected.dtype)
    return mixed_sum

def filter_values(weight_first, biases, sine_rates, middle, weight_last, decay_rate, begin_at, count_rows, length):
    places = jnp.asarray(begin_at).astype(jnp.float32) + jnp.arange(count_rows, dtype=jnp.float32)
    fraction = places / (length - 1)
    band_count = (weight_first.shape[0] - 1) // 2
    band_rates = jnp.linspace(0.0001, band_count - 1, band_count, dtype=jnp.float32)
    phases = 2 * math.pi / length * places
    embedded = jnp.concatenate([fraction[:, None], jnp.cos(band_rates[None, :] * phases[:, None]), -jnp.sin(band_rates[None, :] * phases[:, None])], axis=1)
    hidden = jnp.sin(sine_rates[0] * (jnp.dot(embedded, weight_first, precision=highest) + biases[0]))
    hidden = jnp.sin(sine_rates[1] * (jnp.dot(hidden, middle, precision=highest) + biases[1]))
    return jnp.dot(hidden, weight_last, precision=highest) * jnp.exp(-fraction[:, None] * decay_rate[None, :])

def doc_conv(filter_now, gated, doc_masks):
    length = gated.shape[1]
    spec_filter = jnp.fft.rfft(filter_now, n=2 * length, axis=0)
    conv_sum = jnp.zeros_like(gated)
    for doc_idx in range(doc_masks.shape[-1]):
        doc_mask = doc_masks[..., doc_idx:doc_idx + 1]
        spectra = jnp.fft.rfft(gated * doc_mask, n=2 * length, axis=1)
        conv_sum = conv_sum + doc_mask * jnp.fft.irfft(spectra * spec_filter[None], n=2 * length, axis=1)[:, :length]
    return conv_sum

def forward(stream, segment, doc_masks, params):
    norm_gain, weight_in, short_taps, net_first, net_biases, net_rates, net_middle, net_last, net_decay, skip_weight, weight_out, weight_up, weight_down = params
    length = stream.shape[1]
    model_width = stream.shape[2]
    for layer_at in range(norm_gain.shape[0]):
        filter_now = low(filter_values(net_first[layer_at], net_biases[layer_at], net_rates[layer_at], net_middle[layer_at], net_last[layer_at], net_decay[layer_at], 0, length, length))
        normed = low(layer_norm(stream, norm_gain[layer_at, 0]))
        projected = low_back(jnp.einsum('rld,de->rle', normed, weight_in[layer_at], precision=highest))
        short_out = short_mix(projected, short_taps[layer_at], segment)
        gate_out = short_out[..., :model_width]
        gate_in = short_out[..., model_width:2 * model_width]
        values = short_out[..., 2 * model_width:]
        gated = low(values * gate_in)
        conv_out = low_back(doc_conv(filter_now, gated, doc_masks))
        mixer_out = low((conv_out + gated * skip_weight[layer_at]) * gate_out)
        stream = stream + low_back(jnp.einsum('rld,de->rle', mixer_out, weight_out[layer_at], precision=highest))
        normed_mlp = low(layer_norm(stream, norm_gain[layer_at, 1]))
        up_out = low_back(jnp.einsum('rld,df->rlf', normed_mlp, weight_up[layer_at], precision=highest))
        activated = low(jax.nn.gelu(up_out, approximate=False))
        stream = stream + low_back(jnp.einsum('rlf,fd->rld', activated, weight_down[layer_at], precision=highest))
    return stream

def reference(tokens_in, doc_lengths, norm_gains, in_proj, short_filter, filter_in, filter_biases, sine_freq, filter_mid, filter_out, decay_rates, skip_bias, out_proj, mlp_up, mlp_down, out_grad):
    params = tuple((array_in.astype(jnp.float32) for array_in in (norm_gains, in_proj, short_filter, filter_in, filter_biases, sine_freq, filter_mid, filter_out, decay_rates, skip_bias, out_proj, mlp_up, mlp_down)))
    row_count = tokens_in.shape[0]
    group_rows = 4
    block_count = row_count // group_rows

    def shaped(array_in):
        return array_in.reshape((block_count, group_rows) + array_in.shape[1:])

    def advance(summed_up, inputs):
        tokens, lengths, cotangent = inputs
        segment = segments(lengths, tokens.shape[1])
        doc_masks = (segment[..., None] == jnp.arange(lengths.shape[1], dtype=jnp.int32)).astype(jnp.float32)

        def run_layers(stream, *weights):
            return forward(stream, segment, doc_masks, weights)
        result, pull_back = jax.vjp(run_layers, tokens.astype(jnp.float32), *params)
        gradients = pull_back(cotangent.astype(jnp.float32))
        summed_up = tuple((left + right for left, right in zip(summed_up, gradients[1:])))
        return (summed_up, (result.astype(jnp.bfloat16), gradients[0]))
    begin_sums = tuple((jnp.zeros_like(array_in) for array_in in params))
    summed_up, (outputs, input_grads) = lax.scan(advance, begin_sums, (shaped(tokens_in), shaped(doc_lengths), shaped(out_grad)))
    tokens_out = outputs.reshape(tokens_in.shape)
    tokens_grad = input_grads.reshape(tokens_in.shape)
    return (tokens_out, tokens_grad, summed_up[0], summed_up[1], summed_up[2], summed_up[3], summed_up[4], summed_up[5], summed_up[6], summed_up[7], summed_up[8], summed_up[9], summed_up[10], summed_up[11], summed_up[12])
```

```python
import functools
import math

import jax
import jax.numpy as jnp
import ml_dtypes
import numpy as np
from jax import lax
from jax.experimental import pallas as pl
from jax.experimental.pallas import tpu as pltpu
from jax.sharding import PartitionSpec as P

f32 = jnp.float32
bf16 = jnp.bfloat16
highest = lax.Precision.HIGHEST
norm_epsilon = 1e-05
lanes = 128
vmem_bytes = 56 * 1024 * 1024


def digit_of(name):
    if name in ("z", "c"):
        extent = lax.axis_size("dp")
        return ("dp", extent, 2, extent // 2) if name == "z" else ("dp", extent, 1, 2)
    extent = lax.axis_size("pos")
    return ("pos", extent, extent // 2, 2) if name == "y" else ("pos", extent, 1, extent // 2)


def digit_at(name):
    axis, extent, stride, size = digit_of(name)
    return lax.axis_index(axis) // stride % size


def digit_size(name):
    return digit_of(name)[3]


def hop_along(value, name, hop=1):
    axis, extent, stride, size = digit_of(name)
    perm = []
    for at in range(extent):
        digit = at // stride % size
        perm.append((at, at + ((digit + hop) % size - digit) * stride))
    return lax.ppermute(value, axis, perm)


def core_groups(axis):
    at = np.arange(lax.axis_size(axis))
    span = at.size // lax.axis_size("dp")
    return [list(map(int, at[at // span % 2 == side])) for side in range(2)]


def pass_line(unit):
    pieces = [unit]
    for _ in range(digit_size("z") - 1):
        pieces.append(hop_along(pieces[-1], "z"))
    return pieces


def gather_sides(pieces, order):
    held = jnp.stack(pieces, axis=0)
    sent = {name: hop_along(held, name) for name in order}
    return [held, sent["x"], sent["y"], hop_along(sent[order[0]], order[1])]


def after(value, earlier):
    return lax.optimization_barrier((value, earlier))[0]


def fold_next(keep, got_first):
    return (keep[1].astype(f32) + got_first[1].astype(f32)).astype(bf16)


def fold_line(keep, got_first, got_next):
    total = keep[0].astype(f32) + got_first[0].astype(f32) + got_next.astype(f32)
    return total.astype(bf16)


def ring_line(value):
    size = value.shape[0]
    total, arrived = value[size - 1], []
    for k in range(size - 2, -1, -1):
        arrived.append(hop_along(total.astype(bf16), "z"))
        total = arrived[-1].astype(f32) + value[k].astype(f32)
    return total, arrived


def sum_places(value):
    for axis, step in (("pos", 1), ("dp", 2)):
        extent = lax.axis_size(axis)
        low = value.astype(bf16)
        terms = [low.astype(f32)]
        for bits in range(step, extent, step):
            perm = [(at, at ^ bits) for at in range(extent)]
            terms.append(lax.ppermute(low, axis, perm).astype(f32))
        while len(terms) > 1:
            terms = [terms[k] + terms[k + 1] for k in range(0, len(terms), 2)]
        value = terms[0]
    low = value.astype(bf16)
    return low.astype(f32), hop_along(low, "c").astype(f32)


def embedding(length, width):
    places = np.arange(length, dtype=np.float64)
    bands = (width - 1) // 2
    turns = np.linspace(0.0001, bands - 1, bands)[None, :] * (2 * math.pi / length * places)[:, None]
    table = [places[:, None] / (length - 1), np.cos(turns), -np.sin(turns)]
    return jnp.asarray(np.concatenate(table, axis=1).astype(np.float32))


def filter_states(embedded, weight_first, biases, sine_rates, middle, weight_last, decay_rate):
    length = embedded.shape[0]
    fraction = jnp.arange(length, dtype=f32) / (length - 1)
    inner_one = jnp.dot(embedded, weight_first, precision=highest) + biases[0]
    turn_one = sine_rates[0] * inner_one
    hidden_one = jnp.sin(turn_one)
    inner_two = jnp.dot(hidden_one, middle, precision=highest) + biases[1]
    turn_two = sine_rates[1] * inner_two
    hidden_two = jnp.sin(turn_two)
    values = jnp.dot(hidden_two, weight_last, precision=highest) * jnp.exp(
        -fraction[:, None] * decay_rate[None, :]
    )
    states = (hidden_one, jnp.cos(turn_one), inner_one, hidden_two, jnp.cos(turn_two), inner_two)
    return values, jnp.stack(states, axis=0)


def spectrum_tables(length):
    turns = (2 * np.arange(length)[:, None] + 1) * np.arange(length)[None, :] % (4 * length)
    angles = math.pi / (2 * length) * turns
    table = np.concatenate([np.cos(angles), -np.sin(angles)], axis=0)
    return (
        jnp.asarray(table.astype(ml_dtypes.bfloat16)),
        jnp.asarray((table.T / length).astype(ml_dtypes.bfloat16)),
    )


def dot(left, right):
    return jnp.dot(left, right, preferred_element_type=f32)


def dot_rows(left, right):
    return lax.dot_general(left, right, (((0,), (0,)), ((), ())), preferred_element_type=f32)


def dot_turned(left, right):
    return lax.dot_general(left, right, (((1,), (1,)), ((), ())), preferred_element_type=f32)


def exact_rows(left, right):
    return lax.dot_general(
        left, right, (((0,), (0,)), ((), ())), precision=highest, preferred_element_type=f32
    )


def exact_turned(left, right):
    return lax.dot_general(
        left, right, (((1,), (1,)), ((), ())), precision=highest, preferred_element_type=f32
    )


def normalise(values):
    centered = values - jnp.mean(values, axis=-1, keepdims=True)
    inv_scale = lax.rsqrt(jnp.mean(centered * centered, axis=-1, keepdims=True) + norm_epsilon)
    return centered * inv_scale, inv_scale


def norm_back(stream, gain, grad):
    unit, inv_scale = normalise(stream)
    scaled = grad * gain
    moved = jnp.mean(scaled, axis=-1, keepdims=True)
    along = jnp.mean(scaled * unit, axis=-1, keepdims=True)
    return inv_scale * (scaled - moved - unit * along)


def row_slice(row, length):
    return pl.ds(pl.multiple_of(row * length, length), length)


def doc_places(info, row):
    return info[4 + 3 * row], info[5 + 3 * row], info[6 + 3 * row]


def masks_of(info, row, length, width):
    start_one, start_two, long_from = doc_places(info, row)
    at = lax.broadcasted_iota(jnp.int32, (length, width), 0)
    join_one = (at != 0) & (at != start_one) & (at != start_two)
    join_two = join_one & (at != 1) & (at != start_one + 1) & (at != start_two + 1)
    in_long = (at >= long_from) & (at < long_from + (length - length // 16))
    return join_one, join_two, in_long


def edge_offsets(info, row, length, width):
    small = length // 16
    start_one, start_two, long_from = doc_places(info, row)
    at = lax.broadcasted_iota(jnp.int32, (2 * small, width), 0)
    at = jnp.where(at < small, at, at + (length - 2 * small))
    start = jnp.where(at >= start_two, start_two, jnp.where(at >= start_one, start_one, 0))
    in_long = (at >= long_from) & (at < long_from + (length - small))
    return jnp.where(in_long, -1, at - start)


def edges(values, small):
    return jnp.concatenate([values[:small], values[values.shape[0] - small :]], axis=0)


def start_copies(copies, sems):
    started = []
    for index, (source, target) in enumerate(copies):
        copy = pltpu.make_async_copy(source, target, sems.at[index])
        copy.start()
        started.append(copy)
    return started


def piece_places(info, line, pieces):
    for k in range(line):
        z = lax.rem(info[0] + line - k, line)
        for number in range(4):
            y = (info[1] + number // 2) % 2
            x = (info[2] + number % 2) % 2
            yield pieces[number].at[k], z, y * 2 + x


def joined(piece_ref):
    value = piece_ref[...]
    return value.astype(f32).reshape(-1, value.shape[-1]).astype(bf16)


def unit_copies(info, stage, keep, send, line, order, begin=0):
    copies = []
    blocks = pl.ds(begin, keep.shape[2])
    for far_first in range(2):
        target = send if far_first else keep
        for far_next in range(2):
            far_y, far_x = (far_first, far_next) if order[0] == "y" else (far_next, far_first)
            y = (info[1] + far_y) % 2
            x = (info[2] + far_x) % 2
            for k in range(line):
                z = lax.rem(info[0] + k, line)
                copies.append((stage.at[z, y, x, blocks], target.at[far_next, k]))
    return copies


def mixer_forward(*refs, cfg, first):
    length, half, line = cfg["length"], cfg["half"], cfg["line"]
    refs = list(refs)
    info = refs.pop(0)
    weights = [refs.pop(0) for _ in range(4 if cfg["pieces"] else 2)]
    base_ref = refs.pop(0)
    if not first:
        own_ref, got_ref = refs.pop(0), refs.pop(0)
    gain_ref, taps_ref, skip_ref, filt_ref, fore_ref, back_ref = refs[:6]
    refs = refs[6:]
    stream_out, normed_out, proj_out, short_out, gated_out, summed_out, mixed_out, part_out = refs[:8]
    refs = refs[8:]
    if cfg["pieces"]:
        w_in, w_out = refs.pop(0), refs.pop(0)
        spec_ref, proj_ref, conv_ref, in_pieces, out_pieces, sems = refs
        copies = []
        for piece, z, place in piece_places(info, line, weights):
            for core in range(2):
                copies.append((piece.at[pl.ds(core * 3, 3)], in_pieces.at[:, z, core, place]))
            copies.append((piece.at[pl.ds(6, 2)], out_pieces.at[:, z, place]))
        started = start_copies(copies, sems)
    else:
        w_in, w_out = weights
        spec_ref, proj_ref, conv_ref = refs

    def head(row, carry):
        here, there = row_slice(row, length), row_slice(1 - row, length)
        stream = base_ref[here, :].astype(f32)
        if not first:
            stream = stream + (own_ref[here, :].astype(f32) + got_ref[there, :].astype(f32))
        stream_out[here, :] = stream
        normed_out[here, :] = (normalise(stream)[0] * gain_ref[...]).astype(bf16)
        return carry

    lax.fori_loop(0, 2, head, 0)
    spec_ref[...] = dot(fore_ref[...], filt_ref[...])
    if cfg["pieces"]:
        for copy in started:
            copy.wait()
        for block in range(3):
            w_in[:, block * half : (block + 1) * half] = joined(in_pieces.at[block])
        for block in range(2):
            w_out[:, block * half : (block + 1) * half] = joined(out_pieces.at[block])
    for block in range(3):
        span = slice(block * half, (block + 1) * half)
        proj_ref[:, span] = dot(normed_out[...], w_in[:, span])

    def body(row, carry):
        here = row_slice(row, length)
        join_one, join_two, in_long = masks_of(info, row, length, lanes)
        for tile in range(half // lanes):
            mixed = []
            for block in range(3):
                span = slice(block * half + tile * lanes, block * half + (tile + 1) * lanes)
                values = proj_ref[here, span]
                proj_out[here, span] = values.astype(bf16)
                out = taps_ref[0:1, span] * values
                out = out + taps_ref[1:2, span] * jnp.where(join_one, pltpu.roll(values, 1, 0), 0.0)
                out = out + taps_ref[2:3, span] * jnp.where(join_two, pltpu.roll(values, 2, 0), 0.0)
                short_out[here, span] = out.astype(bf16)
                mixed.append(out)
            span = slice(tile * lanes, (tile + 1) * lanes)
            gated = (mixed[2] * mixed[1]).astype(bf16)
            gated_out[here, span] = gated
            kept = jnp.where(in_long, gated.astype(f32), 0.0).astype(bf16)
            spec = dot(fore_ref[...], kept)
            real, imag = spec[:length], spec[length:]
            f_real, f_imag = spec_ref[:length, span], spec_ref[length:, span]
            prod = jnp.concatenate(
                [real * f_real - imag * f_imag, real * f_imag + imag * f_real], axis=0
            ).astype(bf16)
            conv_ref[:, span] = jnp.where(in_long, dot(back_ref[...], prod), 0.0)
            small = length // 16
            off = edge_offsets(info, row, length, lanes)
            ends = edges(gated.astype(f32), small)
            taps = filt_ref[0:small, span].astype(f32)
            extra = jnp.where(off >= 0, ends, 0.0) * taps[0:1]
            for lag in range(1, small - 1):
                extra = extra + taps[lag : lag + 1] * jnp.where(
                    off >= lag, pltpu.roll(ends, lag, 0), 0.0
                )
            conv_ref[0:small, span] = conv_ref[0:small, span] + extra[:small]
            conv_ref[length - small :, span] = conv_ref[length - small :, span] + extra[small:]
            summed = conv_ref[:, span] + gated.astype(f32) * skip_ref[:, span]
            summed_out[here, span] = summed.astype(bf16)
            mixed_out[here, span] = (summed * mixed[0]).astype(bf16)
        return carry

    lax.fori_loop(0, 2, body, 0)
    part_out[...] = dot(mixed_out[...], w_out[...]).astype(bf16)


def mlp_forward(*refs, cfg):
    length, half, line = cfg["length"], cfg["half"], cfg["line"]
    refs = list(refs)
    info = refs.pop(0)
    weights = [refs.pop(0) for _ in range(8 if cfg["pieces"] else 2)]
    base_ref, own_ref, got_ref, gain_ref = refs[:4]
    stream_out, normed_out, act_out, slope_out, part_out = refs[4:9]
    refs = refs[9:]
    if cfg["pieces"]:
        w_up, w_down = refs.pop(0), refs.pop(0)
        up_ref, sum_ref, up_pieces, down_pieces, sems = refs
        copies = []
        for piece, z, place in piece_places(info, line, weights[:4]):
            for core in range(2):
                copies.append((piece.at[pl.ds(core * 4, 4)], up_pieces.at[:, z, core, place]))
        for piece, z, place in piece_places(info, line, weights[4:]):
            for side in range(2):
                copies.append((piece.at[pl.ds(side * 4, 4)], down_pieces.at[side, z, place]))
        started = start_copies(copies, sems)
    else:
        w_up, w_down = weights
        up_ref, sum_ref = refs

    def head(row, carry):
        here, there = row_slice(row, length), row_slice(1 - row, length)
        stream = base_ref[here, :] + (own_ref[here, :].astype(f32) + got_ref[there, :].astype(f32))
        stream_out[here, :] = stream
        normed_out[here, :] = (normalise(stream)[0] * gain_ref[...]).astype(bf16)
        return carry

    lax.fori_loop(0, 2, head, 0)
    if cfg["pieces"]:
        for copy in started:
            copy.wait()
        for block in range(4):
            w_up[:, block * half : (block + 1) * half] = joined(up_pieces.at[block])
        for side in range(2):
            w_down[:, side * half : (side + 1) * half] = joined(down_pieces.at[side])
    width = w_up.shape[1]
    step = width // 2
    rows = 64
    for part in range(2):
        span = slice(part * step, (part + 1) * step)
        up_ref[...] = dot(normed_out[...], w_up[:, span])

        def bend(at, carry):
            here = row_slice(at, rows)
            values = up_ref[here, :]
            share = 0.5 + 0.5 * lax.erf(values * math.sqrt(0.5))
            bell = jnp.exp(values * values * -0.5) * (1 / math.sqrt(2 * math.pi))
            act_out[here, span] = (values * share).astype(bf16)
            slope_out[here, span] = (share + values * bell).astype(bf16)
            return carry

        lax.fori_loop(0, up_ref.shape[0] // rows, bend, 0)
        product = dot(act_out[:, span], w_down[span, :])
        if part == 0:
            sum_ref[...] = product
        else:
            part_out[...] = (sum_ref[...] + product).astype(bf16)


def grad_head(refs, cfg, stream_grad):
    length = cfg["length"]
    base_ref, own_ref, got_ref, stream_ref, gain_ref = refs

    def head(row, carry):
        here, there = row_slice(row, length), row_slice(1 - row, length)
        grad = own_ref[here, :].astype(f32) + got_ref[there, :].astype(f32)
        moved = norm_back(stream_ref[here, :], gain_ref[...], grad)
        stream_grad[here, :] = base_ref[here, :].astype(f32) + moved
        return carry

    lax.fori_loop(0, 2, head, 0)


def gain_grads_of(stream_ref, part_ref, gain_out, length):
    gain_out[...] = jnp.zeros_like(gain_out)

    def add(row, carry):
        here = row_slice(row, length)
        unit = normalise(stream_ref[here, :])[0]
        grad = part_ref[here, :].astype(f32)
        gain_out[...] += jnp.sum(grad * unit, axis=0, keepdims=True)
        return carry

    lax.fori_loop(0, 2, add, 0)


def mlp_backward(*refs, cfg, top, orders):
    length, half, line = cfg["length"], cfg["half"], cfg["line"]
    refs = list(refs)
    info = refs.pop(0)
    w_up, w_down, normed_ref, act_ref, slope_ref, mid_ref = refs[:6]
    refs = refs[6:]
    if top:
        low = refs.pop(0)
    else:
        inputs = refs[:5]
        refs = refs[5:]
        grad_out = refs.pop(0)
    part_out, gain_out = refs.pop(0), refs.pop(0)
    if cfg["pieces"]:
        up_keep, up_send, down_keep, down_send = refs[:4]
        refs = refs[4:]
    else:
        up_whole, down_whole = refs[:2]
        refs = refs[2:]
    sum_ref = refs.pop(0)
    if not top:
        low = refs.pop(0)
    if cfg["pieces"]:
        up_stage, down_stage, sems = refs
        own = cfg["own"]
    if not top:
        grad_head(inputs, cfg, grad_out)
        low[...] = grad_out[...].astype(bf16)
    width = w_up.shape[1]
    step = width // 2
    started = []
    for part in range(2):
        span = slice(part * step, (part + 1) * step)
        product = dot_rows(act_ref[:, span], low[...])
        if cfg["pieces"]:
            units = product.reshape(line // 2, 4, 4, own, 2 * half)
            for spot in range(2 * line):
                for quarter in range(4):
                    for side in range(2):
                        down_stage[
                            part * line // 2 + spot // 4, spot // 2 % 2, spot % 2, side * 4 + quarter
                        ] = units[
                            spot // 4, spot % 4, quarter, :, side * half : (side + 1) * half
                        ].astype(bf16)
        else:
            down_whole[span, :] = product.astype(bf16)
    if cfg["pieces"]:
        started += start_copies(
            unit_copies(info, down_stage, down_keep, down_send, line, orders[1]), sems.at[0]
        )
    for part in range(2):
        span = slice(part * step, (part + 1) * step)
        grad_up = (dot_turned(low[...], w_down[span, :]) * slope_ref[:, span].astype(f32)).astype(bf16)
        product = dot_rows(normed_ref[...], grad_up)
        if cfg["pieces"]:
            units = product.reshape(line, 2, 2, 2, own, step)
            for z in range(line):
                for spot in range(8):
                    core, y, x = spot // 4, spot // 2 % 2, spot % 2
                    for block in range(2):
                        up_stage[z, y, x, core * 4 + part * 2 + block] = units[
                            z, core, y, x, :, block * half : (block + 1) * half
                        ].astype(bf16)
        else:
            up_whole[:, span] = product.astype(bf16)
        product = dot_turned(grad_up, w_up[:, span])
        if part == 0:
            sum_ref[...] = product
        else:
            part_out[...] = (sum_ref[...] + product).astype(bf16)
    if cfg["pieces"]:
        started += start_copies(
            unit_copies(info, up_stage, up_keep, up_send, line, orders[0]), sems.at[1]
        )
    gain_grads_of(mid_ref, part_out, gain_out, length)
    if cfg["pieces"]:
        for copy in started:
            copy.wait()


def net_backward(grads, refs, decay_ref, small_out):
    embed_ref, states_ref, values_ref, rates_ref, middle_ref, last_ref = refs
    hidden_one, slope_one, inner_one, hidden_two, slope_two, inner_two = (
        states_ref[k] for k in range(6)
    )
    length, wide = grads.shape
    width = middle_ref.shape[0]
    edge = embed_ref.shape[1]
    fraction = lax.broadcasted_iota(jnp.int32, grads.shape, 0).astype(f32) / (length - 1)
    grad_decay = jnp.sum(grads * values_ref[...] * -fraction, axis=0, keepdims=True)
    grads = grads * jnp.exp(-fraction * decay_ref[...])
    small_out[0:width, :] = exact_rows(hidden_two, grads)
    small_out[width : width + 1, :] = grad_decay
    grad_two = exact_turned(grads, last_ref[...]) * slope_two
    rate_two = jnp.sum(grad_two * inner_two, axis=0, keepdims=True)
    grad_two = grad_two * rates_ref[1:2]
    bias_two = jnp.sum(grad_two, axis=0, keepdims=True)
    grad_middle = exact_rows(hidden_one, grad_two)
    grad_one = exact_turned(grad_two, middle_ref[...]) * slope_one
    rate_one = jnp.sum(grad_one * inner_one, axis=0, keepdims=True)
    grad_one = grad_one * rates_ref[0:1]
    bias_one = jnp.sum(grad_one, axis=0, keepdims=True)
    grad_first = exact_rows(embed_ref[...], grad_one)
    base = 80
    rows = width // 2
    small_out[base:, :] = jnp.zeros_like(small_out[base:, :])
    small_out[base : base + rows, 0:width] = grad_middle[:rows]
    small_out[base : base + rows, width : 2 * width] = grad_middle[rows:]
    small_out[base : base + rows, 2 * width : 3 * width] = grad_first[:rows]
    tail = (grad_first[rows:edge], bias_one, bias_two, rate_one, rate_two)
    row = base
    for part in tail:
        small_out[row : row + part.shape[0], 3 * width : 4 * width] = part
        row += part.shape[0]


def mixer_backward(*refs, cfg, orders):
    length, half, line = cfg["length"], cfg["half"], cfg["line"]
    small = length // 16
    refs = list(refs)
    info = refs.pop(0)
    w_in, w_out, normed_ref, proj_ref, short_ref, gated_ref, summed_ref, mixed_ref = refs[:8]
    inputs = refs[8:13]
    taps_ref, skip_ref, filt_ref, fore_ref, back_ref = refs[13:18]
    net_refs = refs[18:24]
    decay_ref, stream_ref = refs[24:26]
    grad_out, gain_out, part_out, small_out = refs[26:30]
    refs = refs[30:]
    if cfg["pieces"]:
        keeps, sends = refs[0:2], refs[2:4]
        refs = refs[4:]
    else:
        in_whole, out_whole = refs.pop(0), refs.pop(0)
    low, mix_ref, spec_ref, acc_ref, edge_ref, gp_ref, gated_grad, skip_out, taps_out, filt_out = refs[:10]
    refs = refs[10:]
    grad_head(inputs, cfg, grad_out)
    low[...] = grad_out[...].astype(bf16)
    mix_ref[...] = dot_turned(low[...], w_out[...])
    spec_ref[...] = dot(fore_ref[...], filt_ref[...])
    acc_ref[...] = jnp.zeros_like(acc_ref)
    edge_ref[...] = jnp.zeros_like(edge_ref)
    skip_out[...] = jnp.zeros_like(skip_out)
    taps_out[...] = jnp.zeros_like(taps_out)

    def body(row, carry):
        here = row_slice(row, length)
        join_one, join_two, in_long = masks_of(info, row, length, lanes)
        for tile in range(half // lanes):
            span = slice(tile * lanes, (tile + 1) * lanes)
            out_span = span
            in_span = slice(half + tile * lanes, half + (tile + 1) * lanes)
            value_span = slice(2 * half + tile * lanes, 2 * half + (tile + 1) * lanes)
            grad_mix = mix_ref[here, span]
            gated = gated_ref[here, span].astype(f32)
            grad_sum = grad_mix * short_ref[here, out_span].astype(f32)
            grad_gate_out = grad_mix * summed_ref[here, span].astype(f32)
            skip_out[:, span] += jnp.sum(grad_sum * gated, axis=0, keepdims=True)
            grad_conv = grad_sum.astype(bf16).astype(f32)
            both = jnp.concatenate(
                [jnp.where(in_long, grad_conv, 0.0), jnp.where(in_long, gated, 0.0)], axis=1
            ).astype(bf16)
            spec = dot(fore_ref[...], both)
            c_real, c_imag = spec[:length, :lanes], spec[length:, :lanes]
            g_real, g_imag = spec[:length, lanes:], spec[length:, lanes:]
            f_real, f_imag = spec_ref[:length, span], spec_ref[length:, span]
            prod = jnp.concatenate(
                [c_real * f_real + c_imag * f_imag, c_imag * f_real - c_real * f_imag], axis=0
            ).astype(bf16)
            acc_ref[:length, span] += c_real * g_real + c_imag * g_imag
            acc_ref[length:, span] += c_imag * g_real - c_real * g_imag
            gated_grad[...] = grad_sum * skip_ref[:, span] + jnp.where(
                in_long, dot(back_ref[...], prod), 0.0
            )
            off = edge_offsets(info, row, length, lanes)
            conv_ends = edges(grad_conv, small)
            gated_ends = edges(gated, small)
            taps = filt_ref[0:small, span].astype(f32)
            extra = jnp.zeros_like(conv_ends)
            for lag in range(small - 1):
                kept = jnp.where(off >= lag, conv_ends, 0.0)
                if lag:
                    extra = extra + taps[lag : lag + 1] * pltpu.roll(kept, 2 * small - lag, 0)
                    kept = kept * pltpu.roll(gated_ends, lag, 0)
                else:
                    extra = extra + taps[0:1] * kept
                    kept = kept * gated_ends
                edge_ref[lag : lag + 1, span] += jnp.sum(kept, axis=0, keepdims=True)
            gated_grad[0:small, :] += extra[:small]
            gated_grad[length - small :, :] += extra[small:]
            grad_gated = gated_grad[...]
            parts = (
                (grad_gate_out, out_span),
                (grad_gated * short_ref[here, value_span].astype(f32), in_span),
                (grad_gated * short_ref[here, in_span].astype(f32), value_span),
            )
            for grad, where in parts:
                values = proj_ref[here, where].astype(f32)
                one = jnp.where(join_one, grad, 0.0)
                two = jnp.where(join_two, grad, 0.0)
                back = taps_ref[0:1, where] * grad
                back = back + taps_ref[1:2, where] * pltpu.roll(one, length - 1, 0)
                back = back + taps_ref[2:3, where] * pltpu.roll(two, length - 2, 0)
                gp_ref[here, where] = back.astype(bf16)
                taps_out[0:1, where] += jnp.sum(grad * values, axis=0, keepdims=True)
                taps_out[1:2, where] += jnp.sum(one * pltpu.roll(values, 1, 0), axis=0, keepdims=True)
                taps_out[2:3, where] += jnp.sum(two * pltpu.roll(values, 2, 0), axis=0, keepdims=True)
        return carry

    lax.fori_loop(0, 2, body, 0)
    high = acc_ref[...].astype(bf16)
    rest = (acc_ref[...] - high.astype(f32)).astype(bf16)
    filt_out[...] = dot(back_ref[...], high) + dot(back_ref[...], rest)
    filt_out[0:small, :] += edge_ref[...]
    net_backward(filt_out[...], net_refs, decay_ref, small_out)
    small_out[65:66, :] = skip_out[...]
    for tap in range(3):
        for block in range(3):
            row = 66 + tap * 3 + block
            small_out[row : row + 1, :] = taps_out[tap : tap + 1, block * half : (block + 1) * half]
    part_out[...] = dot_turned(gp_ref[...], w_in[...]).astype(bf16)
    product = dot_rows(mixed_ref[...], low[...])
    if cfg["pieces"]:
        own = cfg["own"]
        stage, sems = refs
        units = product.reshape(line, 2, 2, own, 2 * half)
        for z in range(line):
            for spot in range(4):
                for side in range(2):
                    stage[z, spot // 2, spot % 2, 6 + side] = units[
                        z, spot // 2, spot % 2, :, side * half : (side + 1) * half
                    ].astype(bf16)
    else:
        out_whole[...] = product.astype(bf16)
    for block in range(3):
        span = slice(block * half, (block + 1) * half)
        product = dot_rows(normed_ref[...], gp_ref[:, span])
        if cfg["pieces"]:
            units = product.reshape(line, 2, 2, 2, own, half)
            for z in range(line):
                for spot in range(8):
                    core, y, x = spot // 4, spot // 2 % 2, spot % 2
                    stage[z, y, x, core * 3 + block] = units[z, core, y, x].astype(bf16)
        else:
            in_whole[:, span] = product.astype(bf16)
    if cfg["pieces"]:
        copies = []
        for number in range(2):
            copies += unit_copies(
                info, stage, keeps[number], sends[number], line, orders[number], number * 4
            )
        started = start_copies(copies, sems)
    gain_grads_of(stream_ref, part_out, gain_out, length)
    if cfg["pieces"]:
        for copy in started:
            copy.wait()


def last_backward(*refs, cfg):
    length = cfg["length"]
    base_ref, own_ref, got_ref, stream_ref, gain_ref, grad_out = refs
    grad = own_ref[0:length, :].astype(f32) + got_ref[length:, :].astype(f32)
    moved = norm_back(stream_ref[0:length, :], gain_ref[...], grad)
    grad_out[...] = base_ref[0:length, :] + moved


def run(body, outs, scratch, info, loose, args, flops, loose_outs=0):
    in_vmem = pl.BlockSpec(memory_space=pltpu.VMEM)
    in_hbm = pl.BlockSpec(memory_space=pl.ANY)
    in_smem = pl.BlockSpec(memory_space=pltpu.SMEM)
    specs = [in_smem] if info is not None else []
    specs += [in_hbm] * len(loose) + [in_vmem] * len(args)
    operands = ([info] if info is not None else []) + list(loose) + list(args)
    moved = sum(a.size * a.dtype.itemsize for a in operands)
    moved += sum(math.prod(o.shape) * o.dtype.itemsize for o in outs)
    return pl.pallas_call(
        body,
        out_shape=outs,
        in_specs=specs,
        out_specs=[in_vmem] * (len(outs) - loose_outs) + [in_hbm] * loose_outs,
        scratch_shapes=scratch,
        compiler_params=pltpu.CompilerParams(vmem_limit_bytes=vmem_bytes),
        cost_estimate=pl.CostEstimate(
            flops=int(flops) // 4096, bytes_accessed=int(moved) // 4096, transcendentals=0
        ),
    )(*operands)


def shape(*sizes, dtype=bf16):
    return jax.ShapeDtypeStruct(sizes, dtype)


def per_device(
    tokens_in,
    doc_lengths,
    norm_gains,
    in_proj,
    short_filter,
    filter_in,
    filter_biases,
    sine_freq,
    filter_mid,
    filter_out,
    decay_rates,
    skip_bias,
    out_proj,
    mlp_up,
    mlp_down,
    out_grad,
):
    length, wide = tokens_in.shape[1:]
    layer_count = norm_gains.shape[0]
    deep = mlp_up.shape[2]
    half, deep_half = wide // 2, deep // 2
    own, own_deep = in_proj.shape[1], mlp_down.shape[1]
    line, pos_size = digit_size("z"), lax.axis_size("pos")
    count = 2 * line * pos_size
    pieces = own % 8 == 0 and pos_size == 4 and line % 2 == 0 and own_deep == 4 * own and line == 4
    cfg = dict(length=length, half=half, line=line, pieces=pieces, own=own)
    core = digit_at("c")
    tokens = 2 * length

    def halves(value, axis):
        cut = value.shape[:axis] + (line, 2, value.shape[axis] // (2 * line)) + value.shape[axis + 1 :]
        return value.reshape(cut)

    def pick(value, axis, which):
        taken = lax.dynamic_index_in_dim(halves(value, axis), which, axis + 1, False)
        return taken.reshape(value.shape[:axis] + (value.shape[axis] // 2,) + value.shape[axis + 1 :])

    def place(mine, other, axis):
        cut = mine.shape[:axis] + (line, mine.shape[axis] // line) + mine.shape[axis + 1 :]
        mine, other = mine.reshape(cut), other.reshape(cut)
        pair = jnp.stack(
            [jnp.where(core == 0, mine, other), jnp.where(core == 0, other, mine)], axis=axis + 1
        )
        whole = cut[:axis] + (cut[axis] * 2 * cut[axis + 1],) + cut[axis + 2 :]
        return pair.reshape(whole)

    pieces_of = []
    if pieces:

        def columns(value, blocks, which):
            part = lax.dynamic_index_in_dim(
                value.reshape(layer_count, own, blocks, line, 2, -1), which, 4, False
            )
            return part.reshape(layer_count, own, -1, half).transpose(0, 2, 1, 3)

        mine = jnp.concatenate([columns(in_proj, 3, core), columns(mlp_up, 1, core)], axis=1)
        theirs = jnp.concatenate([columns(in_proj, 3, 1 - core), columns(mlp_up, 1, 1 - core)], axis=1)
        got = hop_along(theirs, "c")
        low_core = jnp.where(core == 0, mine, got)
        high_core = jnp.where(core == 0, got, mine)
        unit_out = out_proj.reshape(layer_count, own, 2, half).transpose(0, 2, 1, 3)
        unit_down = mlp_down.reshape(layer_count, 4, own, 2, half).transpose(0, 3, 1, 2, 4)
        unit_down = unit_down.reshape(layer_count, 8, own, half)
        units_in = jnp.concatenate([low_core[:, :3], high_core[:, :3], unit_out], axis=1)
        units_up = jnp.concatenate([low_core[:, 3:], high_core[:, 3:]], axis=1)
        chunks = []
        for layer_at in range(layer_count):
            chunks += [units_in[layer_at], units_up[layer_at], unit_down[layer_at]]
        lined = [pass_line(chunks[0]), pass_line(chunks[1])]
        for number in range(2, len(chunks), 2):
            pair = jnp.concatenate(chunks[number : number + 2], axis=0)
            pieces_now = pass_line(after(pair, lined[0][-1] if number == 2 else pieces_now[-1]))
            lined.append([piece[:8] for piece in pieces_now])
            lined.append([piece[8:] for piece in pieces_now])
        held = [
            gather_sides(pieces_now, ("y", "x") if number % 2 else ("x", "y"))
            for number, pieces_now in enumerate(lined)
        ]
        for layer_at in range(layer_count):
            mix_held, up_held, down_held = held[3 * layer_at : 3 * layer_at + 3]
            pieces_of.append((mix_held, up_held + down_held))

    rows_got = hop_along(jnp.stack([tokens_in[0], out_grad[0]], axis=0), "c")
    both_tokens = jnp.concatenate([tokens_in[0], rows_got[0]], axis=0)
    both_grads = jnp.concatenate([out_grad[0], rows_got[1]], axis=0)
    lengths_got = hop_along(doc_lengths.astype(f32), "c").astype(jnp.int32)
    both_lengths = jnp.concatenate([doc_lengths, lengths_got], axis=0)
    start_one = both_lengths[:, 0]
    start_two = start_one + both_lengths[:, 1]
    longest = jnp.max(both_lengths, axis=1)
    long_from = jnp.where(
        both_lengths[:, 0] == longest, 0, jnp.where(both_lengths[:, 1] == longest, start_one, start_two)
    )
    info = jnp.concatenate(
        [
            jnp.stack([digit_at("z"), digit_at("y"), digit_at("x"), core]).astype(jnp.int32),
            jnp.stack([start_one, start_two, long_from], axis=1).reshape(-1),
        ]
    )
    channel_params = jnp.concatenate(
        [
            short_filter.reshape(layer_count, 9, wide),
            filter_out,
            decay_rates[:, None],
            skip_bias[:, None],
        ],
        axis=1,
    )
    net_width = filter_out.shape[1]
    channel_half = pick(channel_params, 2, core)
    taps_half = channel_half[:, :9].reshape(layer_count, 3, 3 * half)
    last_half = channel_half[:, 9 : 9 + net_width]
    decay_half = channel_half[:, 9 + net_width]
    skip_half = channel_half[:, 10 + net_width :]
    fore, back = spectrum_tables(length)

    embedded = embedding(length, filter_in.shape[1])
    if pieces:
        last_half = after(last_half, got)
        filter_in = after(filter_in, got)
    filters, nets = [], []
    for layer_at in range(layer_count):
        values, states = filter_states(
            embedded,
            filter_in[layer_at],
            filter_biases[layer_at],
            sine_freq[layer_at],
            filter_mid[layer_at],
            last_half[layer_at],
            decay_half[layer_at],
        )
        filters.append(values.astype(bf16))
        nets.append(
            [
                embedded,
                states,
                values,
                sine_freq[layer_at],
                filter_mid[layer_at],
                last_half[layer_at],
                decay_half[layer_at][None],
            ]
        )

    dma = pltpu.SemaphoreType.DMA
    saved = []
    base, part, part_got = both_tokens, None, None
    for layer_at in range(layer_count):
        if pieces:
            weights_mix, weights_mlp = pieces_of[layer_at]
        else:

            def whole(value):
                return lax.all_gather(value[layer_at], ("dp", "pos"), axis=0, tiled=True)

            w_in = pick(whole(in_proj).reshape(wide, 3, wide), 2, core).reshape(wide, 3 * half)
            w_out = pick(whole(out_proj), 0, core)
            w_up, w_down = pick(whole(mlp_up), 1, core), pick(whole(mlp_down), 0, core)
            weights_mix, weights_mlp = [w_in, w_out], [w_up, w_down]
        first = layer_at == 0
        outs = [
            shape(tokens, wide, dtype=f32),
            shape(tokens, wide),
            shape(tokens, 3 * half),
            shape(tokens, 3 * half),
            shape(tokens, half),
            shape(tokens, half),
            shape(tokens, half),
            shape(tokens, wide),
        ]
        scratch = [
            pltpu.VMEM((tokens, half), f32),
            pltpu.VMEM((tokens, 3 * half), f32),
            pltpu.VMEM((length, half), f32),
        ]
        if pieces:
            outs += [shape(wide, 3 * half), shape(half, wide)]
            scratch += [
                pltpu.VMEM((3, line, 2, 4, own, half), bf16),
                pltpu.VMEM((2, line, 4, own, half), bf16),
                dma((12 * line,)),
            ]
        streams = [base] if first else [base, part, part_got]
        args = streams + [
            norm_gains[layer_at, 0:1],
            taps_half[layer_at],
            skip_half[layer_at],
            filters[layer_at],
            fore,
            back,
        ]
        result = run(
            functools.partial(mixer_forward, cfg=cfg, first=first),
            outs,
            scratch,
            info,
            weights_mix if pieces else [],
            args if pieces else weights_mix + args,
            2 * tokens * wide * 4 * half,
        )
        stream, normed, proj, short, gated, summed, mixed, part = result[:8]
        if pieces:
            w_in, w_out = result[8:]
        part_got = hop_along(part, "c")
        outs = [
            shape(tokens, wide, dtype=f32),
            shape(tokens, wide),
            shape(tokens, deep_half),
            shape(tokens, deep_half),
            shape(tokens, wide),
        ]
        scratch = [pltpu.VMEM((tokens, deep_half // 2), f32), pltpu.VMEM((tokens, wide), f32)]
        if pieces:
            outs += [shape(wide, deep_half), shape(deep_half, wide)]
            scratch += [
                pltpu.VMEM((4, line, 2, 4, own, half), bf16),
                pltpu.VMEM((2, line, 4, 4, own, half), bf16),
                dma((16 * line,)),
            ]
        args = [stream, part, part_got, norm_gains[layer_at, 1:2]]
        result = run(
            functools.partial(mlp_forward, cfg=cfg),
            outs,
            scratch,
            info,
            weights_mlp if pieces else [],
            args if pieces else weights_mlp + args,
            4 * tokens * wide * deep_half,
        )
        stream_mid, normed_mlp, act, slope, part = result[:5]
        if pieces:
            w_up, w_down = result[5:]
        if layer_at < layer_count - 1:
            part_got = hop_along(part, "c")
        base = stream_mid
        saved.append(
            (
                (w_in, w_out, normed, proj, short, gated, summed, mixed),
                (w_up, w_down, normed_mlp, act, slope),
                stream,
                stream_mid,
            )
        )
    last_part = part

    collected = [None] * layer_count
    grad_base, part, part_got, stream_above, gain_above = both_grads, None, None, None, None
    gain_grads = [[None, None] for _ in range(layer_count)]
    pending, turned = [], []

    def send_folded(group, name, gate):
        ready = [after(got_first, gate) for _, got_first in group]
        value = jnp.concatenate(
            [fold_next(keep, got_first) for (keep, _), got_first in zip(group, ready)], axis=1
        )
        return ready, value, hop_along(value, name)

    def line_terms(group, ready, got_next, gate):
        got_next = after(got_next, gate)
        terms, begin = [], 0
        for (keep, _), got_first in zip(group, ready):
            blocks = keep.shape[2]
            terms.append(fold_line(keep, got_first, got_next[:, begin : begin + blocks]))
            begin += blocks
        return terms

    def owned_parts(sum_down, sum_up, sum_mix):
        by_core = jnp.concatenate(
            [sum_mix[:6].reshape(2, 3, own, half), sum_up.reshape(2, 4, own, half)], axis=1
        )
        ours = lax.dynamic_index_in_dim(by_core, core, 0, False)
        sent = lax.dynamic_index_in_dim(by_core, 1 - core, 0, False)
        theirs = hop_along(sent.astype(bf16), "c").astype(f32)

        def rows_of(blocks, begin, end):
            mine, other = (
                value[begin:end].transpose(1, 0, 2).reshape(own, blocks, line, -1)
                for value in (ours, theirs)
            )
            pair = jnp.stack(
                [jnp.where(core == 0, mine, other), jnp.where(core == 0, other, mine)], axis=3
            )
            return pair.reshape(own, -1)

        return (
            rows_of(3, 0, 3),
            sum_mix[6:].transpose(1, 0, 2).reshape(own, wide),
            rows_of(1, 3, 7),
            sum_down.reshape(2, 4, own, half).transpose(1, 2, 0, 3).reshape(own_deep, wide),
        )

    flip = False
    unit_shape = shape(2, line, 8, own, half)
    half_shape = shape(2, line, 4, own, half)
    stage = pltpu.VMEM((line, 2, 2, 8, own, half), bf16)
    for layer_at in reversed(range(layer_count)):
        mix_saved, mlp_saved, stream, stream_mid = saved[layer_at]
        top = layer_at == layer_count - 1
        orders = (("x", "y"), ("y", "x")) if flip else (("y", "x"), ("x", "y"))
        outs = [] if top else [shape(tokens, wide, dtype=f32)]
        outs += [shape(tokens, wide), shape(1, wide, dtype=f32)]
        scratch = [pltpu.VMEM((tokens, wide), f32)]
        scratch += [] if top else [pltpu.VMEM((tokens, wide), bf16)]
        if pieces:
            outs += [unit_shape] * 4
            scratch += [stage, stage, dma((2, 4 * line))]
        else:
            outs += [shape(wide, deep_half), shape(deep_half, wide)]
        args = list(mlp_saved) + [stream_mid]
        args += [grad_base] if top else [grad_base, part, part_got, stream_above, gain_above]
        result = list(
            run(
                functools.partial(mlp_backward, cfg=cfg, top=top, orders=orders),
                outs,
                scratch,
                info,
                [],
                args,
                8 * tokens * wide * deep_half,
                4 if pieces else 0,
            )
        )
        if not top:
            grad_base = result.pop(0)
        part = result.pop(0)
        gain_grads[layer_at][1] = result.pop(0)
        part_got = hop_along(part, "c")
        mlp_grads = result
        if pieces and not top:
            groups = pending[-1]
            sent_above = [send_folded(groups[name], name, part) for name in ("x", "y")]
            gates = [entry[1] for entry in sent_above]
            mlp_grads[1] = after(mlp_grads[1], gates)
            mlp_grads[3] = after(mlp_grads[3], gates)
        outs = [
            shape(tokens, wide, dtype=f32),
            shape(1, wide, dtype=f32),
            shape(tokens, wide),
            shape(112, half, dtype=f32),
        ]
        scratch = [
            pltpu.VMEM((tokens, wide), bf16),
            pltpu.VMEM((tokens, half), f32),
            pltpu.VMEM((tokens, half), f32),
            pltpu.VMEM((tokens, half), f32),
            pltpu.VMEM((length // 16, half), f32),
            pltpu.VMEM((tokens, 3 * half), bf16),
            pltpu.VMEM((length, lanes), f32),
            pltpu.VMEM((1, half), f32),
            pltpu.VMEM((3, 3 * half), f32),
            pltpu.VMEM((length, half), f32),
        ]
        if pieces:
            outs += [half_shape] * 4
            scratch += [stage, dma((8 * line,))]
        else:
            outs += [shape(wide, 3 * half), shape(half, wide)]
        args = list(mix_saved) + [
            grad_base,
            part,
            part_got,
            stream_mid,
            norm_gains[layer_at, 1:2],
            taps_half[layer_at],
            skip_half[layer_at],
            filters[layer_at],
            fore,
            back,
        ]
        args += nets[layer_at] + [stream]
        result = run(
            functools.partial(mixer_backward, cfg=cfg, orders=orders),
            outs,
            scratch,
            info,
            [],
            args,
            4 * tokens * wide * 4 * half,
            4 if pieces else 0,
        )
        grad_base, gain_grads[layer_at][0], part, small_grads = result[:4]
        if layer_at:
            part_got = hop_along(part, "c")
        mix_grads = result[4:]
        stream_above, gain_above = stream, norm_gains[layer_at, 0:1]
        if pieces:
            groups = {"x": [], "y": []}
            for keep, send, order in (
                (mlp_grads[2], mlp_grads[3], orders[1]),
                (mlp_grads[0], mlp_grads[1], orders[0]),
                (mix_grads[0], mix_grads[2], orders[0]),
                (mix_grads[1], mix_grads[3], orders[1]),
            ):
                groups[order[1]].append((keep, hop_along(send, order[0])))
            pending.append(groups)
            turned.append(orders[1][1] == "x")
            owned = None
        else:

            def owned_of(value, axis):
                full = place(value, jnp.zeros_like(value), axis)
                full = full.reshape(full.shape[0], -1)
                return lax.psum_scatter(full, ("dp", "pos"), scatter_dimension=0, tiled=True).astype(f32)

            owned = (
                owned_of(mix_grads[0].reshape(wide, 3, half), 2),
                owned_of(mix_grads[1], 0),
                owned_of(mlp_grads[0], 1),
                owned_of(mlp_grads[1], 0),
            )
        collected[layer_at] = (owned, small_grads)
        flip = not flip
    all_gains = jnp.concatenate([gain for pair in gain_grads for gain in pair], axis=0)
    all_gains = all_gains.reshape(-1, half)
    small_total = jnp.concatenate([entry[1] for entry in collected] + [all_gains], axis=0)
    part_got = hop_along(part, "c")
    last_got = hop_along(after(last_part, part), "c")
    tokens_out = (
        saved[-1][3][:length] + (last_part[:length].astype(f32) + last_got[length:].astype(f32))
    ).astype(bf16)[None]

    if pieces:
        folded = []
        gate, earlier = part, part
        for groups, flipped in zip(pending, turned):
            if groups is pending[-1]:
                sent_now = [send_folded(groups[name], name, gate) for name in ("x", "y")]
            else:
                sent_now = sent_above
            terms = [
                line_terms(groups[name], entry[0], entry[2], earlier)
                for name, entry in zip(("x", "y"), sent_now)
            ]
            total, arrived = ring_line(jnp.concatenate(terms[0] + terms[1], axis=1))
            gate, earlier = arrived[0], arrived[-1]
            first_part, second_part = total[:12], total[12:]
            down_part, up_part = (first_part, second_part) if flipped else (second_part, first_part)
            sum_mix = jnp.concatenate([up_part[8:], down_part[8:]], axis=0)
            folded.append((down_part[:8], up_part[:8], sum_mix))
        for layer_at in range(layer_count):
            owned = owned_parts(*folded[layer_count - 1 - layer_at])
            collected[layer_at] = (owned, collected[layer_at][1])
    if pieces:
        small_total = after(small_total, gate)
    all_mine, all_other = sum_places(small_total)
    (grad_tokens,) = run(
        functools.partial(last_backward, cfg=cfg),
        [shape(length, wide, dtype=f32)],
        [],
        None,
        [],
        [grad_base, part, part_got, stream_above, gain_above],
        20 * length * wide,
    )
    at = lax.axis_index(("dp", "pos"))
    edge = filter_in.shape[1]
    gains = (all_mine + all_other)[112 * layer_count :].reshape(layer_count, 2, wide)
    sums = []
    for layer_at in range(layer_count):
        mine = all_mine[112 * layer_at : 112 * (layer_at + 1)]
        other = all_other[112 * layer_at : 112 * (layer_at + 1)]
        full = place(mine[:75], other[:75], 1)
        both = mine[80:] + other[80:]
        narrow = both[: net_width // 2]
        tail = narrow[:, 3 * net_width : 4 * net_width]
        rest = edge - net_width // 2

        def owned_small(value):
            share = value.shape[-1] // count
            return lax.dynamic_slice_in_dim(value, at * share, share, value.ndim - 1)

        sums.append(
            (
                jnp.concatenate([narrow[:, 2 * net_width : 3 * net_width], tail[:rest]], axis=0),
                tail[rest : rest + 2],
                tail[rest + 2 : rest + 4],
                jnp.concatenate([narrow[:, :net_width], narrow[:, net_width : 2 * net_width]], axis=0),
                full[:net_width],
                full[net_width],
                None,
                owned_small(full[net_width + 2 : net_width + 11].reshape(3, 3 * wide)),
                owned_small(full[net_width + 1]),
            )
        )

    def stacked(picker):
        return jnp.stack([picker(layer_at) for layer_at in range(layer_count)], axis=0)

    return (
        tokens_out,
        grad_tokens[None],
        owned_small(gains),
        stacked(lambda k: collected[k][0][0]),
        stacked(lambda k: sums[k][7]),
        stacked(lambda k: sums[k][0]),
        stacked(lambda k: sums[k][1]),
        stacked(lambda k: sums[k][2]),
        stacked(lambda k: sums[k][3]),
        stacked(lambda k: sums[k][4]),
        stacked(lambda k: sums[k][5]),
        stacked(lambda k: sums[k][8]),
        stacked(lambda k: collected[k][0][1]),
        stacked(lambda k: collected[k][0][2]),
        stacked(lambda k: collected[k][0][3]),
    )


def solution(mesh):
    rows = P(("dp", "pos"), None, None)
    matrix = P(None, ("dp", "pos"), None)
    last = P(None, None, ("dp", "pos"))
    return jax.shard_map(
        per_device,
        mesh=mesh,
        in_specs=(
            rows,
            P(("dp", "pos"), None),
            P(),
            matrix,
            P(),
            P(),
            P(),
            P(),
            P(),
            P(),
            P(),
            P(),
            matrix,
            matrix,
            matrix,
            rows,
        ),
        out_specs=(
            rows,
            rows,
            last,
            matrix,
            last,
            P(),
            P(),
            P(),
            P(),
            P(),
            P(),
            P(None, ("dp", "pos")),
            matrix,
            matrix,
            matrix,
        ),
        check_vma=False,
    )
```

```python
import functools
import math

import jax
import jax.numpy as jnp
import ml_dtypes
import numpy as np
from jax import lax
from jax.experimental import pallas as pl
from jax.experimental.pallas import tpu as pltpu
from jax.sharding import PartitionSpec as P

f32 = jnp.float32
bf16 = jnp.bfloat16
highest = lax.Precision.HIGHEST
norm_epsilon = 1e-05
lanes = 128
vmem_bytes = 56 * 1024 * 1024


def digit_of(name):
    if name in ("z", "c"):
        extent = lax.axis_size("dp")
        return ("dp", extent, 2, extent // 2) if name == "z" else ("dp", extent, 1, 2)
    extent = lax.axis_size("pos")
    return ("pos", extent, extent // 2, 2) if name == "y" else ("pos", extent, 1, extent // 2)


def digit_at(name):
    axis, extent, stride, size = digit_of(name)
    return lax.axis_index(axis) // stride % size


def digit_size(name):
    return digit_of(name)[3]


def hop_along(value, name, hop=1):
    axis, extent, stride, size = digit_of(name)
    perm = []
    for at in range(extent):
        digit = at // stride % size
        perm.append((at, at + ((digit + hop) % size - digit) * stride))
    return lax.ppermute(value, axis, perm)


def core_groups(axis):
    at = np.arange(lax.axis_size(axis))
    span = at.size // lax.axis_size("dp")
    return [list(map(int, at[at // span % 2 == side])) for side in range(2)]


def pass_line(unit):
    pieces = [unit]
    for _ in range(digit_size("z") - 1):
        pieces.append(hop_along(pieces[-1], "z"))
    return pieces


def gather_sides(pieces, order):
    held = jnp.stack(pieces, axis=0)
    sent = {name: hop_along(held, name) for name in order}
    return [held, sent["x"], sent["y"], hop_along(sent[order[0]], order[1])]


def after(value, earlier):
    return lax.optimization_barrier((value, earlier))[0]


def fold_next(keep, got_first):
    return (keep[1].astype(f32) + got_first[1].astype(f32)).astype(bf16)


def fold_line(keep, got_first, got_next):
    total = keep[0].astype(f32) + got_first[0].astype(f32) + got_next.astype(f32)
    return total.astype(bf16)


def ring_line(value):
    size = value.shape[0]
    total, arrived = value[size - 1], []
    for k in range(size - 2, -1, -1):
        arrived.append(hop_along(total.astype(bf16), "z"))
        total = arrived[-1].astype(f32) + value[k].astype(f32)
    return total, arrived


def sum_places(value):
    for axis, step in (("pos", 1), ("dp", 2)):
        extent = lax.axis_size(axis)
        low = value.astype(bf16)
        terms = [low.astype(f32)]
        for bits in range(step, extent, step):
            perm = [(at, at ^ bits) for at in range(extent)]
            terms.append(lax.ppermute(low, axis, perm).astype(f32))
        while len(terms) > 1:
            terms = [terms[k] + terms[k + 1] for k in range(0, len(terms), 2)]
        value = terms[0]
    low = value.astype(bf16)
    return low.astype(f32), hop_along(low, "c").astype(f32)


def embedding(length, width):
    places = np.arange(length, dtype=np.float64)
    bands = (width - 1) // 2
    turns = np.linspace(0.0001, bands - 1, bands)[None, :] * (2 * math.pi / length * places)[:, None]
    table = [places[:, None] / (length - 1), np.cos(turns), -np.sin(turns)]
    return jnp.asarray(np.concatenate(table, axis=1).astype(np.float32))


def filter_states(embedded, weight_first, biases, sine_rates, middle, weight_last, decay_rate):
    length = embedded.shape[0]
    fraction = jnp.arange(length, dtype=f32) / (length - 1)
    inner_one = jnp.dot(embedded, weight_first, precision=highest) + biases[0]
    turn_one = sine_rates[0] * inner_one
    hidden_one = jnp.sin(turn_one)
    inner_two = jnp.dot(hidden_one, middle, precision=highest) + biases[1]
    turn_two = sine_rates[1] * inner_two
    hidden_two = jnp.sin(turn_two)
    values = jnp.dot(hidden_two, weight_last, precision=highest) * jnp.exp(
        -fraction[:, None] * decay_rate[None, :]
    )
    states = (hidden_one, jnp.cos(turn_one), inner_one, hidden_two, jnp.cos(turn_two), inner_two)
    return values, jnp.stack(states, axis=0)


def spectrum_tables(length):
    turns = (2 * np.arange(length)[:, None] + 1) * np.arange(length)[None, :] % (4 * length)
    angles = math.pi / (2 * length) * turns
    table = np.concatenate([np.cos(angles), -np.sin(angles)], axis=0)
    return (
        jnp.asarray(table.astype(ml_dtypes.bfloat16)),
        jnp.asarray((table.T / length).astype(ml_dtypes.bfloat16)),
    )


def dot(left, right):
    return jnp.dot(left, right, preferred_element_type=f32)


def dot_rows(left, right):
    return lax.dot_general(left, right, (((0,), (0,)), ((), ())), preferred_element_type=f32)


def dot_turned(left, right):
    return lax.dot_general(left, right, (((1,), (1,)), ((), ())), preferred_element_type=f32)


def exact_rows(left, right):
    return lax.dot_general(
        left, right, (((0,), (0,)), ((), ())), precision=highest, preferred_element_type=f32
    )


def exact_turned(left, right):
    return lax.dot_general(
        left, right, (((1,), (1,)), ((), ())), precision=highest, preferred_element_type=f32
    )


def normalise(values):
    centered = values - jnp.mean(values, axis=-1, keepdims=True)
    inv_scale = lax.rsqrt(jnp.mean(centered * centered, axis=-1, keepdims=True) + norm_epsilon)
    return centered * inv_scale, inv_scale


def norm_back(stream, gain, grad):
    unit, inv_scale = normalise(stream)
    scaled = grad * gain
    moved = jnp.mean(scaled, axis=-1, keepdims=True)
    along = jnp.mean(scaled * unit, axis=-1, keepdims=True)
    return inv_scale * (scaled - moved - unit * along)


def row_slice(row, length):
    return pl.ds(pl.multiple_of(row * length, length), length)


def doc_places(info, row):
    return info[4 + 3 * row], info[5 + 3 * row], info[6 + 3 * row]


def masks_of(info, row, length, width):
    start_one, start_two, long_from = doc_places(info, row)
    at = lax.broadcasted_iota(jnp.int32, (length, width), 0)
    join_one = (at != 0) & (at != start_one) & (at != start_two)
    join_two = join_one & (at != 1) & (at != start_one + 1) & (at != start_two + 1)
    in_long = (at >= long_from) & (at < long_from + (length - length // 16))
    return join_one, join_two, in_long


def edge_offsets(info, row, length, width):
    small = length // 16
    start_one, start_two, long_from = doc_places(info, row)
    at = lax.broadcasted_iota(jnp.int32, (2 * small, width), 0)
    at = jnp.where(at < small, at, at + (length - 2 * small))
    start = jnp.where(at >= start_two, start_two, jnp.where(at >= start_one, start_one, 0))
    in_long = (at >= long_from) & (at < long_from + (length - small))
    return jnp.where(in_long, -1, at - start)


def edges(values, small):
    return jnp.concatenate([values[:small], values[values.shape[0] - small :]], axis=0)


def start_copies(copies, sems):
    started = []
    for index, (source, target) in enumerate(copies):
        copy = pltpu.make_async_copy(source, target, sems.at[index])
        copy.start()
        started.append(copy)
    return started


def piece_places(info, line, pieces):
    for k in range(line):
        z = lax.rem(info[0] + line - k, line)
        for number in range(4):
            y = (info[1] + number // 2) % 2
            x = (info[2] + number % 2) % 2
            yield pieces[number].at[k], z, y * 2 + x


def joined(piece_ref):
    value = piece_ref[...]
    return value.astype(f32).reshape(-1, value.shape[-1]).astype(bf16)


def unit_copies(info, stage, keep, send, line, order, begin=0):
    copies = []
    blocks = pl.ds(begin, keep.shape[2])
    for far_first in range(2):
        target = send if far_first else keep
        for far_next in range(2):
            far_y, far_x = (far_first, far_next) if order[0] == "y" else (far_next, far_first)
            y = (info[1] + far_y) % 2
            x = (info[2] + far_x) % 2
            for k in range(line):
                z = lax.rem(info[0] + k, line)
                copies.append((stage.at[z, y, x, blocks], target.at[far_next, k]))
    return copies


def mixer_forward(*refs, cfg, first):
    length, half, line = cfg["length"], cfg["half"], cfg["line"]
    refs = list(refs)
    info = refs.pop(0)
    weights = [refs.pop(0) for _ in range(4 if cfg["pieces"] else 2)]
    base_ref = refs.pop(0)
    if not first:
        own_ref, got_ref = refs.pop(0), refs.pop(0)
    gain_ref, taps_ref, skip_ref, filt_ref, fore_ref, back_ref = refs[:6]
    refs = refs[6:]
    stream_out, normed_out, proj_out, short_out, gated_out, summed_out, mixed_out, part_out = refs[:8]
    refs = refs[8:]
    if cfg["pieces"]:
        w_in, w_out = refs.pop(0), refs.pop(0)
        spec_ref, proj_ref, conv_ref, in_pieces, out_pieces, sems = refs
        copies = []
        for piece, z, place in piece_places(info, line, weights):
            for core in range(2):
                copies.append((piece.at[pl.ds(core * 3, 3)], in_pieces.at[:, z, core, place]))
            copies.append((piece.at[pl.ds(6, 2)], out_pieces.at[:, z, place]))
        started = start_copies(copies, sems)
    else:
        w_in, w_out = weights
        spec_ref, proj_ref, conv_ref = refs

    def head(row, carry):
        here, there = row_slice(row, length), row_slice(1 - row, length)
        stream = base_ref[here, :].astype(f32)
        if not first:
            stream = stream + (own_ref[here, :].astype(f32) + got_ref[there, :].astype(f32))
        stream_out[here, :] = stream
        normed_out[here, :] = (normalise(stream)[0] * gain_ref[...]).astype(bf16)
        return carry

    lax.fori_loop(0, 2, head, 0)
    spec_ref[...] = dot(fore_ref[...], filt_ref[...])
    if cfg["pieces"]:
        for copy in started:
            copy.wait()
        for block in range(3):
            w_in[:, block * half : (block + 1) * half] = joined(in_pieces.at[block])
        for block in range(2):
            w_out[:, block * half : (block + 1) * half] = joined(out_pieces.at[block])
    for block in range(3):
        span = slice(block * half, (block + 1) * half)
        proj_ref[:, span] = dot(normed_out[...], w_in[:, span])

    def body(row, carry):
        here = row_slice(row, length)
        join_one, join_two, in_long = masks_of(info, row, length, lanes)
        for tile in range(half // lanes):
            mixed = []
            for block in range(3):
                span = slice(block * half + tile * lanes, block * half + (tile + 1) * lanes)
                values = proj_ref[here, span]
                proj_out[here, span] = values.astype(bf16)
                out = taps_ref[0:1, span] * values
                out = out + taps_ref[1:2, span] * jnp.where(join_one, pltpu.roll(values, 1, 0), 0.0)
                out = out + taps_ref[2:3, span] * jnp.where(join_two, pltpu.roll(values, 2, 0), 0.0)
                short_out[here, span] = out.astype(bf16)
                mixed.append(out)
            span = slice(tile * lanes, (tile + 1) * lanes)
            gated = (mixed[2] * mixed[1]).astype(bf16)
            gated_out[here, span] = gated
            kept = jnp.where(in_long, gated.astype(f32), 0.0).astype(bf16)
            spec = dot(fore_ref[...], kept)
            real, imag = spec[:length], spec[length:]
            f_real, f_imag = spec_ref[:length, span], spec_ref[length:, span]
            prod = jnp.concatenate(
                [real * f_real - imag * f_imag, real * f_imag + imag * f_real], axis=0
            ).astype(bf16)
            conv_ref[:, span] = jnp.where(in_long, dot(back_ref[...], prod), 0.0)
            small = length // 16
            off = edge_offsets(info, row, length, lanes)
            ends = edges(gated.astype(f32), small)
            taps = filt_ref[0:small, span].astype(f32)
            extra = jnp.where(off >= 0, ends, 0.0) * taps[0:1]
            for lag in range(1, small - 1):
                extra = extra + taps[lag : lag + 1] * jnp.where(
                    off >= lag, pltpu.roll(ends, lag, 0), 0.0
                )
            conv_ref[0:small, span] = conv_ref[0:small, span] + extra[:small]
            conv_ref[length - small :, span] = conv_ref[length - small :, span] + extra[small:]
            summed = conv_ref[:, span] + gated.astype(f32) * skip_ref[:, span]
            summed_out[here, span] = summed.astype(bf16)
            mixed_out[here, span] = (summed * mixed[0]).astype(bf16)
        return carry

    lax.fori_loop(0, 2, body, 0)
    part_out[...] = dot(mixed_out[...], w_out[...]).astype(bf16)


def mlp_forward(*refs, cfg):
    length, half, line = cfg["length"], cfg["half"], cfg["line"]
    refs = list(refs)
    info = refs.pop(0)
    weights = [refs.pop(0) for _ in range(8 if cfg["pieces"] else 2)]
    base_ref, own_ref, got_ref, gain_ref = refs[:4]
    stream_out, normed_out, act_out, slope_out, part_out = refs[4:9]
    refs = refs[9:]
    if cfg["pieces"]:
        w_up, w_down = refs.pop(0), refs.pop(0)
        up_ref, sum_ref, up_pieces, down_pieces, sems = refs
        copies = []
        for piece, z, place in piece_places(info, line, weights[:4]):
            for core in range(2):
                copies.append((piece.at[pl.ds(core * 4, 4)], up_pieces.at[:, z, core, place]))
        for piece, z, place in piece_places(info, line, weights[4:]):
            for side in range(2):
                copies.append((piece.at[pl.ds(side * 4, 4)], down_pieces.at[side, z, place]))
        started = start_copies(copies, sems)
    else:
        w_up, w_down = weights
        up_ref, sum_ref = refs

    def head(row, carry):
        here, there = row_slice(row, length), row_slice(1 - row, length)
        stream = base_ref[here, :] + (own_ref[here, :].astype(f32) + got_ref[there, :].astype(f32))
        stream_out[here, :] = stream
        normed_out[here, :] = (normalise(stream)[0] * gain_ref[...]).astype(bf16)
        return carry

    lax.fori_loop(0, 2, head, 0)
    if cfg["pieces"]:
        for copy in started:
            copy.wait()
        for block in range(4):
            w_up[:, block * half : (block + 1) * half] = joined(up_pieces.at[block])
        for side in range(2):
            w_down[:, side * half : (side + 1) * half] = joined(down_pieces.at[side])
    width = w_up.shape[1]
    step = width // 2
    rows = 64
    for part in range(2):
        span = slice(part * step, (part + 1) * step)
        up_ref[...] = dot(normed_out[...], w_up[:, span])

        def bend(at, carry):
            here = row_slice(at, rows)
            values = up_ref[here, :]
            share = 0.5 + 0.5 * lax.erf(values * math.sqrt(0.5))
            bell = jnp.exp(values * values * -0.5) * (1 / math.sqrt(2 * math.pi))
            act_out[here, span] = (values * share).astype(bf16)
            slope_out[here, span] = (share + values * bell).astype(bf16)
            return carry

        lax.fori_loop(0, up_ref.shape[0] // rows, bend, 0)
        product = dot(act_out[:, span], w_down[span, :])
        if part == 0:
            sum_ref[...] = product
        else:
            part_out[...] = (sum_ref[...] + product).astype(bf16)


def grad_head(refs, cfg, stream_grad):
    length = cfg["length"]
    base_ref, own_ref, got_ref, stream_ref, gain_ref = refs

    def head(row, carry):
        here, there = row_slice(row, length), row_slice(1 - row, length)
        grad = own_ref[here, :].astype(f32) + got_ref[there, :].astype(f32)
        moved = norm_back(stream_ref[here, :], gain_ref[...], grad)
        stream_grad[here, :] = base_ref[here, :].astype(f32) + moved
        return carry

    lax.fori_loop(0, 2, head, 0)


def gain_grads_of(stream_ref, part_ref, gain_out, length):
    gain_out[...] = jnp.zeros_like(gain_out)

    def add(row, carry):
        here = row_slice(row, length)
        unit = normalise(stream_ref[here, :])[0]
        grad = part_ref[here, :].astype(f32)
        gain_out[...] += jnp.sum(grad * unit, axis=0, keepdims=True)
        return carry

    lax.fori_loop(0, 2, add, 0)


def mlp_backward(*refs, cfg, top, orders):
    length, half, line = cfg["length"], cfg["half"], cfg["line"]
    refs = list(refs)
    info = refs.pop(0)
    w_up, w_down, normed_ref, act_ref, slope_ref, mid_ref = refs[:6]
    refs = refs[6:]
    if top:
        low = refs.pop(0)
    else:
        inputs = refs[:5]
        refs = refs[5:]
        grad_out = refs.pop(0)
    part_out, gain_out = refs.pop(0), refs.pop(0)
    if cfg["pieces"]:
        up_keep, up_send, down_keep, down_send = refs[:4]
        refs = refs[4:]
    else:
        up_whole, down_whole = refs[:2]
        refs = refs[2:]
    sum_ref = refs.pop(0)
    if not top:
        low = refs.pop(0)
    if cfg["pieces"]:
        up_stage, down_stage, sems = refs
        own = cfg["own"]
    if not top:
        grad_head(inputs, cfg, grad_out)
        low[...] = grad_out[...].astype(bf16)
    width = w_up.shape[1]
    step = width // 2
    started = []
    for part in range(2):
        span = slice(part * step, (part + 1) * step)
        product = dot_rows(act_ref[:, span], low[...])
        if cfg["pieces"]:
            units = product.reshape(line // 2, 4, 4, own, 2 * half)
            for spot in range(2 * line):
                for quarter in range(4):
                    for side in range(2):
                        down_stage[
                            part * line // 2 + spot // 4, spot // 2 % 2, spot % 2, side * 4 + quarter
                        ] = units[
                            spot // 4, spot % 4, quarter, :, side * half : (side + 1) * half
                        ].astype(bf16)
        else:
            down_whole[span, :] = product.astype(bf16)
    if cfg["pieces"]:
        started += start_copies(
            unit_copies(info, down_stage, down_keep, down_send, line, orders[1]), sems.at[0]
        )
    for part in range(2):
        span = slice(part * step, (part + 1) * step)
        grad_up = (dot_turned(low[...], w_down[span, :]) * slope_ref[:, span].astype(f32)).astype(bf16)
        product = dot_rows(normed_ref[...], grad_up)
        if cfg["pieces"]:
            units = product.reshape(line, 2, 2, 2, own, step)
            for z in range(line):
                for spot in range(8):
                    core, y, x = spot // 4, spot // 2 % 2, spot % 2
                    for block in range(2):
                        up_stage[z, y, x, core * 4 + part * 2 + block] = units[
                            z, core, y, x, :, block * half : (block + 1) * half
                        ].astype(bf16)
        else:
            up_whole[:, span] = product.astype(bf16)
        product = dot_turned(grad_up, w_up[:, span])
        if part == 0:
            sum_ref[...] = product
        else:
            part_out[...] = (sum_ref[...] + product).astype(bf16)
    if cfg["pieces"]:
        started += start_copies(
            unit_copies(info, up_stage, up_keep, up_send, line, orders[0]), sems.at[1]
        )
    gain_grads_of(mid_ref, part_out, gain_out, length)
    if cfg["pieces"]:
        for copy in started:
            copy.wait()


def net_backward(grads, refs, decay_ref, small_out):
    embed_ref, states_ref, values_ref, rates_ref, middle_ref, last_ref = refs
    hidden_one, slope_one, inner_one, hidden_two, slope_two, inner_two = (
        states_ref[k] for k in range(6)
    )
    length, wide = grads.shape
    width = middle_ref.shape[0]
    edge = embed_ref.shape[1]
    fraction = lax.broadcasted_iota(jnp.int32, grads.shape, 0).astype(f32) / (length - 1)
    grad_decay = jnp.sum(grads * values_ref[...] * -fraction, axis=0, keepdims=True)
    grads = grads * jnp.exp(-fraction * decay_ref[...])
    small_out[0:width, :] = exact_rows(hidden_two, grads)
    small_out[width : width + 1, :] = grad_decay
    grad_two = exact_turned(grads, last_ref[...]) * slope_two
    rate_two = jnp.sum(grad_two * inner_two, axis=0, keepdims=True)
    grad_two = grad_two * rates_ref[1:2]
    bias_two = jnp.sum(grad_two, axis=0, keepdims=True)
    grad_middle = exact_rows(hidden_one, grad_two)
    grad_one = exact_turned(grad_two, middle_ref[...]) * slope_one
    rate_one = jnp.sum(grad_one * inner_one, axis=0, keepdims=True)
    grad_one = grad_one * rates_ref[0:1]
    bias_one = jnp.sum(grad_one, axis=0, keepdims=True)
    grad_first = exact_rows(embed_ref[...], grad_one)
    base = 80
    rows = width // 2
    small_out[base:, :] = jnp.zeros_like(small_out[base:, :])
    small_out[base : base + rows, 0:width] = grad_middle[:rows]
    small_out[base : base + rows, width : 2 * width] = grad_middle[rows:]
    small_out[base : base + rows, 2 * width : 3 * width] = grad_first[:rows]
    tail = (grad_first[rows:edge], bias_one, bias_two, rate_one, rate_two)
    row = base
    for part in tail:
        small_out[row : row + part.shape[0], 3 * width : 4 * width] = part
        row += part.shape[0]


def mixer_backward(*refs, cfg, orders):
    length, half, line = cfg["length"], cfg["half"], cfg["line"]
    small = length // 16
    refs = list(refs)
    info = refs.pop(0)
    w_in, w_out, normed_ref, proj_ref, short_ref, gated_ref, summed_ref, mixed_ref = refs[:8]
    inputs = refs[8:13]
    taps_ref, skip_ref, filt_ref, fore_ref, back_ref = refs[13:18]
    net_refs = refs[18:24]
    decay_ref, stream_ref = refs[24:26]
    grad_out, gain_out, part_out, small_out = refs[26:30]
    refs = refs[30:]
    if cfg["pieces"]:
        keeps, sends = refs[0:2], refs[2:4]
        refs = refs[4:]
    else:
        in_whole, out_whole = refs.pop(0), refs.pop(0)
    low, mix_ref, spec_ref, acc_ref, edge_ref, gp_ref, gated_grad, skip_out, taps_out, filt_out = refs[:10]
    refs = refs[10:]
    grad_head(inputs, cfg, grad_out)
    low[...] = grad_out[...].astype(bf16)
    mix_ref[...] = dot_turned(low[...], w_out[...])
    spec_ref[...] = dot(fore_ref[...], filt_ref[...])
    acc_ref[...] = jnp.zeros_like(acc_ref)
    edge_ref[...] = jnp.zeros_like(edge_ref)
    skip_out[...] = jnp.zeros_like(skip_out)
    taps_out[...] = jnp.zeros_like(taps_out)

    def body(row, carry):
        here = row_slice(row, length)
        join_one, join_two, in_long = masks_of(info, row, length, lanes)
        for tile in range(half // lanes):
            span = slice(tile * lanes, (tile + 1) * lanes)
            out_span = span
            in_span = slice(half + tile * lanes, half + (tile + 1) * lanes)
            value_span = slice(2 * half + tile * lanes, 2 * half + (tile + 1) * lanes)
            grad_mix = mix_ref[here, span]
            gated = gated_ref[here, span].astype(f32)
            grad_sum = grad_mix * short_ref[here, out_span].astype(f32)
            grad_gate_out = grad_mix * summed_ref[here, span].astype(f32)
            skip_out[:, span] += jnp.sum(grad_sum * gated, axis=0, keepdims=True)
            grad_conv = grad_sum.astype(bf16).astype(f32)
            both = jnp.concatenate(
                [jnp.where(in_long, grad_conv, 0.0), jnp.where(in_long, gated, 0.0)], axis=1
            ).astype(bf16)
            spec = dot(fore_ref[...], both)
            c_real, c_imag = spec[:length, :lanes], spec[length:, :lanes]
            g_real, g_imag = spec[:length, lanes:], spec[length:, lanes:]
            f_real, f_imag = spec_ref[:length, span], spec_ref[length:, span]
            prod = jnp.concatenate(
                [c_real * f_real + c_imag * f_imag, c_imag * f_real - c_real * f_imag], axis=0
            ).astype(bf16)
            acc_ref[:length, span] += c_real * g_real + c_imag * g_imag
            acc_ref[length:, span] += c_imag * g_real - c_real * g_imag
            gated_grad[...] = grad_sum * skip_ref[:, span] + jnp.where(
                in_long, dot(back_ref[...], prod), 0.0
            )
            off = edge_offsets(info, row, length, lanes)
            conv_ends = edges(grad_conv, small)
            gated_ends = edges(gated, small)
            taps = filt_ref[0:small, span].astype(f32)
            extra = jnp.zeros_like(conv_ends)
            for lag in range(small - 1):
                kept = jnp.where(off >= lag, conv_ends, 0.0)
                if lag:
                    extra = extra + taps[lag : lag + 1] * pltpu.roll(kept, 2 * small - lag, 0)
                    kept = kept * pltpu.roll(gated_ends, lag, 0)
                else:
                    extra = extra + taps[0:1] * kept
                    kept = kept * gated_ends
                edge_ref[lag : lag + 1, span] += jnp.sum(kept, axis=0, keepdims=True)
            gated_grad[0:small, :] += extra[:small]
            gated_grad[length - small :, :] += extra[small:]
            grad_gated = gated_grad[...]
            parts = (
                (grad_gate_out, out_span),
                (grad_gated * short_ref[here, value_span].astype(f32), in_span),
                (grad_gated * short_ref[here, in_span].astype(f32), value_span),
            )
            for grad, where in parts:
                values = proj_ref[here, where].astype(f32)
                one = jnp.where(join_one, grad, 0.0)
                two = jnp.where(join_two, grad, 0.0)
                back = taps_ref[0:1, where] * grad
                back = back + taps_ref[1:2, where] * pltpu.roll(one, length - 1, 0)
                back = back + taps_ref[2:3, where] * pltpu.roll(two, length - 2, 0)
                gp_ref[here, where] = back.astype(bf16)
                taps_out[0:1, where] += jnp.sum(grad * values, axis=0, keepdims=True)
                taps_out[1:2, where] += jnp.sum(one * pltpu.roll(values, 1, 0), axis=0, keepdims=True)
                taps_out[2:3, where] += jnp.sum(two * pltpu.roll(values, 2, 0), axis=0, keepdims=True)
        return carry

    lax.fori_loop(0, 2, body, 0)
    high = acc_ref[...].astype(bf16)
    rest = (acc_ref[...] - high.astype(f32)).astype(bf16)
    filt_out[...] = dot(back_ref[...], high) + dot(back_ref[...], rest)
    filt_out[0:small, :] += edge_ref[...]
    net_backward(filt_out[...], net_refs, decay_ref, small_out)
    small_out[65:66, :] = skip_out[...]
    for tap in range(3):
        for block in range(3):
            row = 66 + tap * 3 + block
            small_out[row : row + 1, :] = taps_out[tap : tap + 1, block * half : (block + 1) * half]
    part_out[...] = dot_turned(gp_ref[...], w_in[...]).astype(bf16)
    product = dot_rows(mixed_ref[...], low[...])
    if cfg["pieces"]:
        own = cfg["own"]
        stage, sems = refs
        units = product.reshape(line, 2, 2, own, 2 * half)
        for z in range(line):
            for spot in range(4):
                for side in range(2):
                    stage[z, spot // 2, spot % 2, 6 + side] = units[
                        z, spot // 2, spot % 2, :, side * half : (side + 1) * half
                    ].astype(bf16)
    else:
        out_whole[...] = product.astype(bf16)
    for block in range(3):
        span = slice(block * half, (block + 1) * half)
        product = dot_rows(normed_ref[...], gp_ref[:, span])
        if cfg["pieces"]:
            units = product.reshape(line, 2, 2, 2, own, half)
            for z in range(line):
                for spot in range(8):
                    core, y, x = spot // 4, spot // 2 % 2, spot % 2
                    stage[z, y, x, core * 3 + block] = units[z, core, y, x].astype(bf16)
        else:
            in_whole[:, span] = product.astype(bf16)
    if cfg["pieces"]:
        copies = []
        for number in range(2):
            copies += unit_copies(
                info, stage, keeps[number], sends[number], line, orders[number], number * 4
            )
        started = start_copies(copies, sems)
    gain_grads_of(stream_ref, part_out, gain_out, length)
    if cfg["pieces"]:
        for copy in started:
            copy.wait()


def last_backward(*refs, cfg):
    length = cfg["length"]
    base_ref, own_ref, got_ref, stream_ref, gain_ref, grad_out = refs
    grad = own_ref[0:length, :].astype(f32) + got_ref[length:, :].astype(f32)
    moved = norm_back(stream_ref[0:length, :], gain_ref[...], grad)
    grad_out[...] = base_ref[0:length, :] + moved


def run(body, outs, scratch, info, loose, args, flops, loose_outs=0):
    in_vmem = pl.BlockSpec(memory_space=pltpu.VMEM)
    in_hbm = pl.BlockSpec(memory_space=pl.ANY)
    in_smem = pl.BlockSpec(memory_space=pltpu.SMEM)
    specs = [in_smem] if info is not None else []
    specs += [in_hbm] * len(loose) + [in_vmem] * len(args)
    operands = ([info] if info is not None else []) + list(loose) + list(args)
    moved = sum(a.size * a.dtype.itemsize for a in operands)
    moved += sum(math.prod(o.shape) * o.dtype.itemsize for o in outs)
    return pl.pallas_call(
        body,
        out_shape=outs,
        in_specs=specs,
        out_specs=[in_vmem] * (len(outs) - loose_outs) + [in_hbm] * loose_outs,
        scratch_shapes=scratch,
        compiler_params=pltpu.CompilerParams(vmem_limit_bytes=vmem_bytes),
        cost_estimate=pl.CostEstimate(
            flops=int(flops) // 4096, bytes_accessed=int(moved) // 4096, transcendentals=0
        ),
    )(*operands)


def shape(*sizes, dtype=bf16):
    return jax.ShapeDtypeStruct(sizes, dtype)


def per_device(
    tokens_in,
    doc_lengths,
    norm_gains,
    in_proj,
    short_filter,
    filter_in,
    filter_biases,
    sine_freq,
    filter_mid,
    filter_out,
    decay_rates,
    skip_bias,
    out_proj,
    mlp_up,
    mlp_down,
    out_grad,
):
    length, wide = tokens_in.shape[1:]
    layer_count = norm_gains.shape[0]
    deep = mlp_up.shape[2]
    half, deep_half = wide // 2, deep // 2
    own, own_deep = in_proj.shape[1], mlp_down.shape[1]
    line, pos_size = digit_size("z"), lax.axis_size("pos")
    count = 2 * line * pos_size
    pieces = own % 8 == 0 and pos_size == 4 and line % 2 == 0 and own_deep == 4 * own and line == 4
    cfg = dict(length=length, half=half, line=line, pieces=pieces, own=own)
    core = digit_at("c")
    tokens = 2 * length

    def halves(value, axis):
        cut = value.shape[:axis] + (line, 2, value.shape[axis] // (2 * line)) + value.shape[axis + 1 :]
        return value.reshape(cut)

    def pick(value, axis, which):
        taken = lax.dynamic_index_in_dim(halves(value, axis), which, axis + 1, False)
        return taken.reshape(value.shape[:axis] + (value.shape[axis] // 2,) + value.shape[axis + 1 :])

    def place(mine, other, axis):
        cut = mine.shape[:axis] + (line, mine.shape[axis] // line) + mine.shape[axis + 1 :]
        mine, other = mine.reshape(cut), other.reshape(cut)
        pair = jnp.stack(
            [jnp.where(core == 0, mine, other), jnp.where(core == 0, other, mine)], axis=axis + 1
        )
        whole = cut[:axis] + (cut[axis] * 2 * cut[axis + 1],) + cut[axis + 2 :]
        return pair.reshape(whole)

    pieces_of = []
    if pieces:

        def columns(value, blocks, which):
            part = lax.dynamic_index_in_dim(
                value.reshape(layer_count, own, blocks, line, 2, -1), which, 4, False
            )
            return part.reshape(layer_count, own, -1, half).transpose(0, 2, 1, 3)

        mine = jnp.concatenate([columns(in_proj, 3, core), columns(mlp_up, 1, core)], axis=1)
        theirs = jnp.concatenate([columns(in_proj, 3, 1 - core), columns(mlp_up, 1, 1 - core)], axis=1)
        got = hop_along(theirs, "c")
        low_core = jnp.where(core == 0, mine, got)
        high_core = jnp.where(core == 0, got, mine)
        unit_out = out_proj.reshape(layer_count, own, 2, half).transpose(0, 2, 1, 3)
        unit_down = mlp_down.reshape(layer_count, 4, own, 2, half).transpose(0, 3, 1, 2, 4)
        unit_down = unit_down.reshape(layer_count, 8, own, half)
        units_in = jnp.concatenate([low_core[:, :3], high_core[:, :3], unit_out], axis=1)
        units_up = jnp.concatenate([low_core[:, 3:], high_core[:, 3:]], axis=1)
        chunks = []
        for layer_at in range(layer_count):
            chunks += [units_in[layer_at], units_up[layer_at], unit_down[layer_at]]
        lined = [pass_line(chunks[0]), pass_line(chunks[1])]
        for number in range(2, len(chunks), 2):
            pair = jnp.concatenate(chunks[number : number + 2], axis=0)
            pieces_now = pass_line(after(pair, lined[0][-1] if number == 2 else pieces_now[-1]))
            lined.append([piece[:8] for piece in pieces_now])
            lined.append([piece[8:] for piece in pieces_now])
        held = [
            gather_sides(pieces_now, ("y", "x") if number % 2 else ("x", "y"))
            for number, pieces_now in enumerate(lined)
        ]
        for layer_at in range(layer_count):
            mix_held, up_held, down_held = held[3 * layer_at : 3 * layer_at + 3]
            pieces_of.append((mix_held, up_held + down_held))

    rows_got = hop_along(jnp.stack([tokens_in[0], out_grad[0]], axis=0), "c")
    both_tokens = jnp.concatenate([tokens_in[0], rows_got[0]], axis=0)
    both_grads = jnp.concatenate([out_grad[0], rows_got[1]], axis=0)
    lengths_got = hop_along(doc_lengths.astype(f32), "c").astype(jnp.int32)
    both_lengths = jnp.concatenate([doc_lengths, lengths_got], axis=0)
    start_one = both_lengths[:, 0]
    start_two = start_one + both_lengths[:, 1]
    longest = jnp.max(both_lengths, axis=1)
    long_from = jnp.where(
        both_lengths[:, 0] == longest, 0, jnp.where(both_lengths[:, 1] == longest, start_one, start_two)
    )
    info = jnp.concatenate(
        [
            jnp.stack([digit_at("z"), digit_at("y"), digit_at("x"), core]).astype(jnp.int32),
            jnp.stack([start_one, start_two, long_from], axis=1).reshape(-1),
        ]
    )
    channel_params = jnp.concatenate(
        [
            short_filter.reshape(layer_count, 9, wide),
            filter_out,
            decay_rates[:, None],
            skip_bias[:, None],
        ],
        axis=1,
    )
    net_width = filter_out.shape[1]
    channel_half = pick(channel_params, 2, core)
    taps_half = channel_half[:, :9].reshape(layer_count, 3, 3 * half)
    last_half = channel_half[:, 9 : 9 + net_width]
    decay_half = channel_half[:, 9 + net_width]
    skip_half = channel_half[:, 10 + net_width :]
    fore, back = spectrum_tables(length)

    embedded = embedding(length, filter_in.shape[1])
    if pieces:
        last_half = after(last_half, got)
        filter_in = after(filter_in, got)
    filters, nets = [], []
    for layer_at in range(layer_count):
        values, states = filter_states(
            embedded,
            filter_in[layer_at],
            filter_biases[layer_at],
            sine_freq[layer_at],
            filter_mid[layer_at],
            last_half[layer_at],
            decay_half[layer_at],
        )
        filters.append(values.astype(bf16))
        nets.append(
            [
                embedded,
                states,
                values,
                sine_freq[layer_at],
                filter_mid[layer_at],
                last_half[layer_at],
                decay_half[layer_at][None],
            ]
        )

    dma = pltpu.SemaphoreType.DMA
    saved = []
    base, part, part_got = both_tokens, None, None
    for layer_at in range(layer_count):
        if pieces:
            weights_mix, weights_mlp = pieces_of[layer_at]
        else:

            def whole(value):
                return lax.all_gather(value[layer_at], ("dp", "pos"), axis=0, tiled=True)

            w_in = pick(whole(in_proj).reshape(wide, 3, wide), 2, core).reshape(wide, 3 * half)
            w_out = pick(whole(out_proj), 0, core)
            w_up, w_down = pick(whole(mlp_up), 1, core), pick(whole(mlp_down), 0, core)
            weights_mix, weights_mlp = [w_in, w_out], [w_up, w_down]
        first = layer_at == 0
        outs = [
            shape(tokens, wide, dtype=f32),
            shape(tokens, wide),
            shape(tokens, 3 * half),
            shape(tokens, 3 * half),
            shape(tokens, half),
            shape(tokens, half),
            shape(tokens, half),
            shape(tokens, wide),
        ]
        scratch = [
            pltpu.VMEM((tokens, half), f32),
            pltpu.VMEM((tokens, 3 * half), f32),
            pltpu.VMEM((length, half), f32),
        ]
        if pieces:
            outs += [shape(wide, 3 * half), shape(half, wide)]
            scratch += [
                pltpu.VMEM((3, line, 2, 4, own, half), bf16),
                pltpu.VMEM((2, line, 4, own, half), bf16),
                dma((12 * line,)),
            ]
        streams = [base] if first else [base, part, part_got]
        args = streams + [
            norm_gains[layer_at, 0:1],
            taps_half[layer_at],
            skip_half[layer_at],
            filters[layer_at],
            fore,
            back,
        ]
        result = run(
            functools.partial(mixer_forward, cfg=cfg, first=first),
            outs,
            scratch,
            info,
            weights_mix if pieces else [],
            args if pieces else weights_mix + args,
            2 * tokens * wide * 4 * half,
        )
        stream, normed, proj, short, gated, summed, mixed, part = result[:8]
        if pieces:
            w_in, w_out = result[8:]
        part_got = hop_along(part, "c")
        outs = [
            shape(tokens, wide, dtype=f32),
            shape(tokens, wide),
            shape(tokens, deep_half),
            shape(tokens, deep_half),
            shape(tokens, wide),
        ]
        scratch = [pltpu.VMEM((tokens, deep_half // 2), f32), pltpu.VMEM((tokens, wide), f32)]
        if pieces:
            outs += [shape(wide, deep_half), shape(deep_half, wide)]
            scratch += [
                pltpu.VMEM((4, line, 2, 4, own, half), bf16),
                pltpu.VMEM((2, line, 4, 4, own, half), bf16),
                dma((16 * line,)),
            ]
        args = [stream, part, part_got, norm_gains[layer_at, 1:2]]
        result = run(
            functools.partial(mlp_forward, cfg=cfg),
            outs,
            scratch,
            info,
            weights_mlp if pieces else [],
            args if pieces else weights_mlp + args,
            4 * tokens * wide * deep_half,
        )
        stream_mid, normed_mlp, act, slope, part = result[:5]
        if pieces:
            w_up, w_down = result[5:]
        if layer_at < layer_count - 1:
            part_got = hop_along(part, "c")
        base = stream_mid
        saved.append(
            (
                (w_in, w_out, normed, proj, short, gated, summed, mixed),
                (w_up, w_down, normed_mlp, act, slope),
                stream,
                stream_mid,
            )
        )
    last_part = part

    collected = [None] * layer_count
    grad_base, part, part_got, stream_above, gain_above = both_grads, None, None, None, None
    gain_grads = [[None, None] for _ in range(layer_count)]
    pending, turned = [], []

    def send_folded(group, name, gate):
        ready = [after(got_first, gate) for _, got_first in group]
        value = jnp.concatenate(
            [fold_next(keep, got_first) for (keep, _), got_first in zip(group, ready)], axis=1
        )
        return ready, value, hop_along(value, name)

    def line_terms(group, ready, got_next, gate):
        got_next = after(got_next, gate)
        terms, begin = [], 0
        for (keep, _), got_first in zip(group, ready):
            blocks = keep.shape[2]
            terms.append(fold_line(keep, got_first, got_next[:, begin : begin + blocks]))
            begin += blocks
        return terms

    def owned_parts(sum_down, sum_up, sum_mix):
        by_core = jnp.concatenate(
            [sum_mix[:6].reshape(2, 3, own, half), sum_up.reshape(2, 4, own, half)], axis=1
        )
        ours = lax.dynamic_index_in_dim(by_core, core, 0, False)
        sent = lax.dynamic_index_in_dim(by_core, 1 - core, 0, False)
        theirs = hop_along(sent.astype(bf16), "c").astype(f32)

        def rows_of(blocks, begin, end):
            mine, other = (
                value[begin:end].transpose(1, 0, 2).reshape(own, blocks, line, -1)
                for value in (ours, theirs)
            )
            pair = jnp.stack(
                [jnp.where(core == 0, mine, other), jnp.where(core == 0, other, mine)], axis=3
            )
            return pair.reshape(own, -1)

        return (
            rows_of(3, 0, 3),
            sum_mix[6:].transpose(1, 0, 2).reshape(own, wide),
            rows_of(1, 3, 7),
            sum_down.reshape(2, 4, own, half).transpose(1, 2, 0, 3).reshape(own_deep, wide),
        )

    flip = False
    unit_shape = shape(2, line, 8, own, half)
    half_shape = shape(2, line, 4, own, half)
    stage = pltpu.VMEM((line, 2, 2, 8, own, half), bf16)
    for layer_at in reversed(range(layer_count)):
        mix_saved, mlp_saved, stream, stream_mid = saved[layer_at]
        top = layer_at == layer_count - 1
        orders = (("x", "y"), ("y", "x")) if flip else (("y", "x"), ("x", "y"))
        outs = [] if top else [shape(tokens, wide, dtype=f32)]
        outs += [shape(tokens, wide), shape(1, wide, dtype=f32)]
        scratch = [pltpu.VMEM((tokens, wide), f32)]
        scratch += [] if top else [pltpu.VMEM((tokens, wide), bf16)]
        if pieces:
            outs += [unit_shape] * 4
            scratch += [stage, stage, dma((2, 4 * line))]
        else:
            outs += [shape(wide, deep_half), shape(deep_half, wide)]
        args = list(mlp_saved) + [stream_mid]
        args += [grad_base] if top else [grad_base, part, part_got, stream_above, gain_above]
        result = list(
            run(
                functools.partial(mlp_backward, cfg=cfg, top=top, orders=orders),
                outs,
                scratch,
                info,
                [],
                args,
                8 * tokens * wide * deep_half,
                4 if pieces else 0,
            )
        )
        if not top:
            grad_base = result.pop(0)
        part = result.pop(0)
        gain_grads[layer_at][1] = result.pop(0)
        part_got = hop_along(part, "c")
        mlp_grads = result
        if pieces and not top:
            groups = pending[-1]
            sent_above = [send_folded(groups[name], name, part) for name in ("x", "y")]
            gates = [entry[1] for entry in sent_above]
            mlp_grads[1] = after(mlp_grads[1], gates)
            mlp_grads[3] = after(mlp_grads[3], gates)
        outs = [
            shape(tokens, wide, dtype=f32),
            shape(1, wide, dtype=f32),
            shape(tokens, wide),
            shape(112, half, dtype=f32),
        ]
        scratch = [
            pltpu.VMEM((tokens, wide), bf16),
            pltpu.VMEM((tokens, half), f32),
            pltpu.VMEM((tokens, half), f32),
            pltpu.VMEM((tokens, half), f32),
            pltpu.VMEM((length // 16, half), f32),
            pltpu.VMEM((tokens, 3 * half), bf16),
            pltpu.VMEM((length, lanes), f32),
            pltpu.VMEM((1, half), f32),
            pltpu.VMEM((3, 3 * half), f32),
            pltpu.VMEM((length, half), f32),
        ]
        if pieces:
            outs += [half_shape] * 4
            scratch += [stage, dma((8 * line,))]
        else:
            outs += [shape(wide, 3 * half), shape(half, wide)]
        args = list(mix_saved) + [
            grad_base,
            part,
            part_got,
            stream_mid,
            norm_gains[layer_at, 1:2],
            taps_half[layer_at],
            skip_half[layer_at],
            filters[layer_at],
            fore,
            back,
        ]
        args += nets[layer_at] + [stream]
        result = run(
            functools.partial(mixer_backward, cfg=cfg, orders=orders),
            outs,
            scratch,
            info,
            [],
            args,
            4 * tokens * wide * 4 * half,
            4 if pieces else 0,
        )
        grad_base, gain_grads[layer_at][0], part, small_grads = result[:4]
        if layer_at:
            part_got = hop_along(part, "c")
        mix_grads = result[4:]
        stream_above, gain_above = stream, norm_gains[layer_at, 0:1]
        if pieces:
            groups = {"x": [], "y": []}
            for keep, send, order in (
                (mlp_grads[2], mlp_grads[3], orders[1]),
                (mlp_grads[0], mlp_grads[1], orders[0]),
                (mix_grads[0], mix_grads[2], orders[0]),
                (mix_grads[1], mix_grads[3], orders[1]),
            ):
                groups[order[1]].append((keep, hop_along(send, order[0])))
            pending.append(groups)
            turned.append(orders[1][1] == "x")
            owned = None
        else:

            def owned_of(value, axis):
                full = place(value, jnp.zeros_like(value), axis)
                full = full.reshape(full.shape[0], -1)
                return lax.psum_scatter(full, ("dp", "pos"), scatter_dimension=0, tiled=True).astype(f32)

            owned = (
                owned_of(mix_grads[0].reshape(wide, 3, half), 2),
                owned_of(mix_grads[1], 0),
                owned_of(mlp_grads[0], 1),
                owned_of(mlp_grads[1], 0),
            )
        collected[layer_at] = (owned, small_grads)
        flip = not flip
    all_gains = jnp.concatenate([gain for pair in gain_grads for gain in pair], axis=0)
    all_gains = all_gains.reshape(-1, half)
    small_total = jnp.concatenate([entry[1] for entry in collected] + [all_gains], axis=0)
    part_got = hop_along(part, "c")
    last_got = hop_along(after(last_part, part), "c")
    tokens_out = (
        saved[-1][3][:length] + (last_part[:length].astype(f32) + last_got[length:].astype(f32))
    ).astype(bf16)[None]

    if pieces:
        folded = []
        gate, earlier = part, part
        for groups, flipped in zip(pending, turned):
            if groups is pending[-1]:
                sent_now = [send_folded(groups[name], name, gate) for name in ("x", "y")]
            else:
                sent_now = sent_above
            terms = [
                line_terms(groups[name], entry[0], entry[2], earlier)
                for name, entry in zip(("x", "y"), sent_now)
            ]
            total, arrived = ring_line(jnp.concatenate(terms[0] + terms[1], axis=1))
            if groups is not pending[-1]:
                gate, earlier = arrived[0], arrived[-1]
            first_part, second_part = total[:12], total[12:]
            down_part, up_part = (first_part, second_part) if flipped else (second_part, first_part)
            sum_mix = jnp.concatenate([up_part[8:], down_part[8:]], axis=0)
            folded.append((down_part[:8], up_part[:8], sum_mix))
        for layer_at in range(layer_count):
            owned = owned_parts(*folded[layer_count - 1 - layer_at])
            collected[layer_at] = (owned, collected[layer_at][1])
    if pieces:
        small_total = after(small_total, earlier)
    all_mine, all_other = sum_places(small_total)
    (grad_tokens,) = run(
        functools.partial(last_backward, cfg=cfg),
        [shape(length, wide, dtype=f32)],
        [],
        None,
        [],
        [grad_base, part, part_got, stream_above, gain_above],
        20 * length * wide,
    )
    at = lax.axis_index(("dp", "pos"))
    edge = filter_in.shape[1]
    gains = (all_mine + all_other)[112 * layer_count :].reshape(layer_count, 2, wide)
    sums = []
    for layer_at in range(layer_count):
        mine = all_mine[112 * layer_at : 112 * (layer_at + 1)]
        other = all_other[112 * layer_at : 112 * (layer_at + 1)]
        full = place(mine[:75], other[:75], 1)
        both = mine[80:] + other[80:]
        narrow = both[: net_width // 2]
        tail = narrow[:, 3 * net_width : 4 * net_width]
        rest = edge - net_width // 2

        def owned_small(value):
            share = value.shape[-1] // count
            return lax.dynamic_slice_in_dim(value, at * share, share, value.ndim - 1)

        sums.append(
            (
                jnp.concatenate([narrow[:, 2 * net_width : 3 * net_width], tail[:rest]], axis=0),
                tail[rest : rest + 2],
                tail[rest + 2 : rest + 4],
                jnp.concatenate([narrow[:, :net_width], narrow[:, net_width : 2 * net_width]], axis=0),
                full[:net_width],
                full[net_width],
                None,
                owned_small(full[net_width + 2 : net_width + 11].reshape(3, 3 * wide)),
                owned_small(full[net_width + 1]),
            )
        )

    def stacked(picker):
        return jnp.stack([picker(layer_at) for layer_at in range(layer_count)], axis=0)

    return (
        tokens_out,
        grad_tokens[None],
        owned_small(gains),
        stacked(lambda k: collected[k][0][0]),
        stacked(lambda k: sums[k][7]),
        stacked(lambda k: sums[k][0]),
        stacked(lambda k: sums[k][1]),
        stacked(lambda k: sums[k][2]),
        stacked(lambda k: sums[k][3]),
        stacked(lambda k: sums[k][4]),
        stacked(lambda k: sums[k][5]),
        stacked(lambda k: sums[k][8]),
        stacked(lambda k: collected[k][0][1]),
        stacked(lambda k: collected[k][0][2]),
        stacked(lambda k: collected[k][0][3]),
    )


def solution(mesh):
    rows = P(("dp", "pos"), None, None)
    matrix = P(None, ("dp", "pos"), None)
    last = P(None, None, ("dp", "pos"))
    return jax.shard_map(
        per_device,
        mesh=mesh,
        in_specs=(
            rows,
            P(("dp", "pos"), None),
            P(),
            matrix,
            P(),
            P(),
            P(),
            P(),
            P(),
            P(),
            P(),
            P(),
            matrix,
            matrix,
            matrix,
            rows,
        ),
        out_specs=(
            rows,
            rows,
            last,
            matrix,
            last,
            P(),
            P(),
            P(),
            P(),
            P(),
            P(),
            P(None, ("dp", "pos")),
            matrix,
            matrix,
            matrix,
        ),
        check_vma=False,
    )
```
